32 devices in a mesh: latent: 8 (over z, core), blk: 4 (over y, x).
Axes of the slice: x: 2, y: 2, z: 4, core: 2. Of those that a mesh axis runs over, the one named last changes fastest.
Arguments:
- activations: bfloat16 [4096, 8192], P(('latent', 'blk')), may hold values from -90 to 90
- block_ids: int32 [4096, 1], P(('latent', 'blk')), may hold values from 0 to 7; in each aligned block of 128 rows (0 to 127, 128 to 255, ...) at most 16 rows name the same one
- enc_weight: bfloat16 [8, 8192, 128], P('latent'), may hold values from -0.0625 to 0.0625
- enc_bias: float32 [8, 128], P('latent'), may hold values from -3 to 3
- dec_weight: bfloat16 [8, 128, 8192], P('latent'), may hold values from -0.5 to 0.5
- dec_bias: float32 [8192], replicated, may hold values from -5 to 5
Outputs:
- recon_loss: float32 [], replicated
- latent_codes: bfloat16 [4096, 128], P(('latent', 'blk'))
- dec_weight_grad: float32 [8, 128, 8192], P('latent', None, 'blk')
The draws below stay inside these ranges and needn't reach their ends.
Inputs may be any that keep to these rules, and one draw needn't show every extreme that they name: `block_ids`: among the rows of one device, every block number is named by exactly 16 rows.
All inputs are finite; a program needn't handle non-finite values.
Results may differ from the reference program's by a relative error of at most 0.0095.
Values may be sent and summed in bfloat16 or wider, within the bound.
A program may use at most 64 MiB of HBM per device.

```python
import math
import jax
import jax.numpy as jnp
import numpy as np
from jax import lax

D = 8192
BW = 128
TOK_DEV = 128
BLOCKS = 8
CAP = 16
TOKENS = 4096


def draw_activations(key, part):
    key_rows, key_cols, key_base = jax.random.split(key, 3)
    position = jnp.arange(TOKENS, dtype=jnp.float32) / TOKENS
    row_scale = 3.0 ** (0.5 * position) * 10.0 ** jax.random.uniform(key_rows, (TOKENS,), jnp.float32, -0.5, 0.5)
    col_scale = 10.0 ** jax.random.uniform(key_cols, (D,), jnp.float32, -0.5, 0.5)
    base = jnp.clip(jax.random.normal(key_base, (TOKENS, D), jnp.float32), -5.0, 5.0)
    return (base * row_scale[:, None] * col_scale[None, :]).astype(jnp.bfloat16)


def block_scale(own_key, extent, cuts, smallest, largest):
    loudness, own = 1.0, jax.random.fold_in(own_key, 6)
    for axis_at, parts in cuts:
        steps = jnp.exp(jax.random.uniform(jax.random.fold_in(own, axis_at), (parts,), jnp.float32, smallest / len(cuts), largest / len(cuts)))
        loudness = loudness * jnp.repeat(steps, extent[axis_at] // parts).reshape([-1 if axis == axis_at else 1 for axis in range(len(extent))])
    return loudness


def routed_block(stream_key, own, number, rows, amount, top, bound, skew):
    ranking = jax.random.permutation(stream_key, amount)
    packed, usual = shares(amount, rows * top, bound, skew, True), shares(amount, rows * top, bound, skew, False)
    places = jnp.arange(amount)

    def named(sizes, offset_by):
        used = int((sizes > 0).sum())
        fixed = max(1, used // 4)
        shifted = fixed + (places - fixed + offset_by * (used - fixed)) % max(1, amount - fixed)
        return jnp.zeros((amount,), jnp.int32).at[ranking[jnp.where(places < fixed, places, shifted)]].set(jnp.asarray(sizes, jnp.int32))

    sizes = jnp.where(number % 4 == 0, named(packed, number // 4), named(usual, number - number // 4 - 1))
    mixed = jax.random.permutation(jax.random.fold_in(own, 3), amount)
    giver, taker = mixed[0:amount // 2 * 2:2], mixed[1:amount // 2 * 2:2]
    slack = jnp.minimum(sizes[giver] - 1, bound - sizes[taker]) // 2
    slack = jnp.where((giver == ranking[0]) | (taker == ranking[0]) | (sizes[taker] == 0), 0, jnp.maximum(slack, 0))
    shifted = jax.random.randint(jax.random.fold_in(own, 4), (amount // 2,), 0, 1 << 20) % (slack + 1)
    sizes = sizes.at[giver].add(-shifted).at[taker].add(shifted)
    labels = jnp.searchsorted(jnp.cumsum(sizes), jnp.arange(rows * top), side="right").astype(jnp.int32)
    grid = labels.reshape(top, rows).T
    grid = grid[jax.random.permutation(jax.random.fold_in(own, 1), rows)]
    offset_by = jax.random.randint(jax.random.fold_in(own, 2), (rows, 1), 0, top)
    return jnp.take_along_axis(grid, (jnp.arange(top)[None, :] + offset_by) % top, axis=1)


def shares(number_of, total, limit, lean, full):
    loads = [(1 << 20) // math.isqrt(rank ** lean) + 1 for rank in range(1, number_of + 1)]
    largest = limit if full else min(limit, max(-(-total // number_of), total * loads[0] // sum(loads)))
    least = 1 if total - largest >= number_of - 1 else 0
    holding, spare = [largest] + [least] * (number_of - 1), total - largest - least * (number_of - 1)
    while spare > 0:
        movable = [i for i in range(1, number_of) if holding[i] < largest] or [i for i in range(1, number_of) if holding[i] < limit]
        pool, budget = sum([loads[i] for i in movable]), spare
        for i in movable:
            addition = min(limit - holding[i], max(1, budget * loads[i] // pool), spare)
            holding[i] = holding[i] + addition
            spare = spare - addition
    return np.array(holding)


def scatter_about(stream_key, shape, deviation, most, pieces=(), held_as=jnp.bfloat16):
    entries = jax.random.normal(stream_key, shape, jnp.float32) * deviation
    if len(pieces) > 0:
        entries = block_scale(stream_key, shape, pieces, -0.22, 0.18) * entries
    return jnp.clip(entries, min=-most, max=most).astype(held_as)


def setup_inputs(seed: int = 0) -> dict:
    arg_keys = jax.random.split(jax.random.key(seed), 7)
    activations = draw_activations(jax.random.fold_in(arg_keys[6], 71), 0)
    block_ids_keys = jax.random.split(jax.random.fold_in(arg_keys[1], 1), TOKENS // TOK_DEV)
    block_ids_turns = jax.random.permutation(jax.random.fold_in(arg_keys[1], 3), TOKENS // TOK_DEV)
    block_ids = jax.vmap(lambda own, number: routed_block(jax.random.fold_in(arg_keys[1], 2), own, number, TOK_DEV, BLOCKS, 1, CAP, 0))(block_ids_keys, block_ids_turns).reshape((TOKENS, 1))
    enc_weight = scatter_about(arg_keys[2], (BLOCKS, D, BW), D ** -0.5, 0.0625, ((0, 8),))
    enc_bias = scatter_about(arg_keys[3], (BLOCKS, BW), 0.5, 3.0, ((0, 8),), jnp.float32)
    dec_weight = scatter_about(arg_keys[4], (BLOCKS, BW, D), BW ** -0.5, 0.5, ((0, 8),))
    dec_bias = scatter_about(arg_keys[5], (D,), 1.0, 5.0, (), jnp.float32)
    return {"activations": activations, "block_ids": block_ids, "enc_weight": enc_weight, "enc_bias": enc_bias, "dec_weight": dec_weight, "dec_bias": dec_bias}


def reference(activations, block_ids, enc_weight, enc_bias, dec_weight, dec_bias):
    block_of = block_ids[:, 0]
    sorted_rows = jnp.argsort(block_of, stable=True).astype(jnp.int32)
    grouped = activations[sorted_rows].reshape(BLOCKS, TOKENS // BLOCKS, D)

    def per_block(inputs):
        rows_in, encoder, bias_in, decoder = inputs
        centered = (rows_in.astype(jnp.float32) - dec_bias).astype(jnp.bfloat16)
        pre_codes = jnp.dot(centered, encoder, preferred_element_type=jnp.float32) + bias_in
        codes = jnp.maximum(pre_codes, 0.0).astype(jnp.bfloat16)
        error_rows = jnp.dot(codes, decoder, preferred_element_type=jnp.float32) + dec_bias - rows_in.astype(jnp.float32)
        squares = jnp.sum(error_rows * error_rows)
        gradient = jnp.dot(codes.T, error_rows.astype(jnp.bfloat16), preferred_element_type=jnp.float32) / (TOKENS // BLOCKS)
        return codes, squares, gradient

    codes, squares, gradient = lax.map(per_block, (grouped, enc_weight, enc_bias, dec_weight))
    inverse = jnp.zeros((TOKENS,), jnp.int32).at[sorted_rows].set(jnp.arange(TOKENS, dtype=jnp.int32))
    latent_codes = codes.reshape(TOKENS, BW)[inverse]
    recon_loss = jnp.sum(squares) / (TOKENS * D)
    return recon_loss, latent_codes, gradient
```

```python
import functools

import jax
import jax.numpy as jnp
from jax import lax
from jax.experimental import pallas as pl
from jax.experimental.pallas import tpu as pltpu
from jax.sharding import PartitionSpec as P

MESH = pl.DeviceIdType.MESH


def flip(index, mask):
    out, bit = index, 1
    while bit <= mask:
        if mask & bit:
            out = out + bit * (1 - 2 * ((index // bit) % 2))
        bit *= 2
    return out


def kernel(
    groups,
    replicas,
    tile,
    ids_ref,
    enc_bias_ref,
    dec_bias_ref,
    act_hbm,
    enc_hbm,
    dec_hbm,
    loss_ref,
    codes_out_ref,
    grad_ref,
    act,
    ordered,
    arrived,
    enc,
    dec,
    parts,
    codes,
    returned,
    squares,
    losses,
    load_sem,
    row_send,
    row_recv,
    part_send,
    part_recv,
    code_send,
    code_recv,
    loss_send,
    loss_recv,
):
    lat, blk = lax.axis_index("latent"), lax.axis_index("blk")
    tok_rows, features = act.shape
    seg = tok_rows // groups
    width = features // replicas
    latents = enc.shape[1]
    tiles = width // tile
    group_rows = 2 * replicas * seg
    own_cols = pl.multiple_of(blk * width, width)
    pairs = [(groups // 2 + i, groups // 2 - 1 - i) for i in range(groups // 2)]
    peers = [(j, e) for j in range(groups) for e in range(replicas) if (j, e) != (0, 0)]

    def device(j, e):
        return (flip(lat, j), flip(blk, e))

    barrier = pltpu.get_barrier_semaphore()
    loads = []
    for e in range(replicas):
        cols = pl.ds(pl.multiple_of(flip(blk, e) * width, width), width)
        loads.append(
            pltpu.make_async_copy(act_hbm.at[:, cols], act.at[:, cols], load_sem.at[e])
        )
    load_enc = pltpu.make_async_copy(
        enc_hbm.at[0, pl.ds(own_cols, width), :], enc, load_sem.at[replicas]
    )
    load_dec = pltpu.make_async_copy(
        dec_hbm.at[0, :, pl.ds(own_cols, width)], dec, load_sem.at[replicas + 1]
    )
    for load in loads:
        load.start()
    for j, e in peers:
        pl.semaphore_signal(barrier, inc=1, device_id=device(j, e), device_id_type=MESH)
    load_enc.start()
    load_dec.start()

    ids = ids_ref[...]
    named = ids == lax.broadcasted_iota(jnp.int32, (tok_rows, 128), 1)
    lower = lax.broadcasted_iota(jnp.int32, (tok_rows, tok_rows), 0) > lax.broadcasted_iota(
        jnp.int32, (tok_rows, tok_rows), 1
    )
    named_f = named.astype(jnp.float32)
    earlier = jnp.dot(
        lower.astype(jnp.float32).astype(jnp.bfloat16),
        named_f.astype(jnp.bfloat16),
        preferred_element_type=jnp.float32,
    )
    place = jnp.sum(named_f * earlier, axis=1, keepdims=True) + ids.astype(jnp.float32) * seg
    spot = lax.broadcasted_iota(jnp.int32, (tok_rows, tok_rows), 1).astype(jnp.float32)
    to_token = (place == spot).astype(jnp.float32)
    to_place = to_token.T.astype(jnp.bfloat16)

    for e in range(replicas):
        loads[e].wait()

        def order_rows(i, carry):
            cols = pl.ds(pl.multiple_of(flip(blk, e) * width + i * tile, tile), tile)
            ordered[:, cols] = jnp.dot(
                to_place, act[:, cols], preferred_element_type=jnp.float32
            ).astype(jnp.bfloat16)
            return carry

        lax.fori_loop(0, tiles, order_rows, 0)

    pl.semaphore_wait(barrier, len(peers))

    row_copies = {}
    for pair_at, pair in enumerate(pairs):
        for e in range(replicas):
            for side, j in enumerate(pair):
                owner, column = device(j, e)
                source = ordered.at[
                    pl.ds(pl.multiple_of(owner * seg, seg), seg),
                    pl.ds(pl.multiple_of(column * width, width), width),
                ]
                slot = (2 * pair_at + side) * replicas + blk
                target = arrived.at[pl.ds(pl.multiple_of(slot * seg, seg), seg), :]
                if (j, e) == (0, 0):
                    copy = pltpu.make_async_copy(source, target, row_recv.at[0])
                else:
                    copy = pltpu.make_async_remote_copy(
                        src_ref=source,
                        dst_ref=target,
                        send_sem=row_send.at[j * replicas + e],
                        recv_sem=row_recv.at[j * replicas + e],
                        device_id=(owner, column),
                        device_id_type=MESH,
                    )
                copy.start()
                row_copies[j, e] = copy

    load_enc.wait()
    load_dec.wait()
    squares[...] = jnp.zeros_like(squares)
    part_copies, code_copies = [], []

    def encode(pair_at):
        for e in range(replicas):
            for j in pairs[pair_at]:
                if (j, e) == (0, 0):
                    row_copies[j, e].wait()
                else:
                    row_copies[j, e].wait_recv()

        def step(i, total):
            cols = pl.ds(pl.multiple_of(i * tile, tile), tile)
            bias = dec_bias_ref[:, pl.ds(pl.multiple_of(own_cols + i * tile, tile), tile)]
            rows = arrived[pl.ds(pair_at * group_rows, group_rows), cols]
            centered = (rows.astype(jnp.float32) - bias).astype(jnp.bfloat16)
            return total + jnp.dot(centered, enc[cols, :], preferred_element_type=jnp.float32)

        parts[pair_at, blk] = lax.fori_loop(
            0, tiles, step, jnp.zeros((group_rows, latents), jnp.float32)
        )
        for e in range(1, replicas):
            copy = pltpu.make_async_remote_copy(
                src_ref=parts.at[pair_at, blk],
                dst_ref=parts.at[pair_at, blk],
                send_sem=part_send.at[pair_at * replicas + e],
                recv_sem=part_recv.at[pair_at * replicas + e],
                device_id=device(0, e),
                device_id_type=MESH,
            )
            copy.start()
            part_copies.append(copy)

    def decode(pair_at):
        for copy in part_copies[pair_at * (replicas - 1) : (pair_at + 1) * (replicas - 1)]:
            copy.wait_recv()
        total = parts[pair_at, 0]
        for d in range(1, replicas):
            total = total + parts[pair_at, d]
        wide = jnp.maximum(total + enc_bias_ref[...], 0.0)
        low = wide.astype(jnp.bfloat16)
        flipped = low.astype(jnp.float32).T.astype(jnp.bfloat16)
        codes[pl.ds(pair_at * group_rows, group_rows), :] = low
        home = pl.ds(pl.multiple_of(lat * seg, seg), seg)
        for side, j in enumerate(pairs[pair_at]):
            slot = (2 * pair_at + side) * replicas + blk
            source = codes.at[pl.ds(pl.multiple_of(slot * seg, seg), seg), :]
            if j == 0:
                copy = pltpu.make_async_copy(source, returned.at[home, :], code_recv.at[0])
            else:
                copy = pltpu.make_async_remote_copy(
                    src_ref=source,
                    dst_ref=returned.at[home, :],
                    send_sem=code_send.at[j],
                    recv_sem=code_recv.at[j],
                    device_id=device(j, 0),
                    device_id_type=MESH,
                )
            copy.start()
            code_copies.append((j, copy))

        def step(i, carry):
            cols = pl.ds(pl.multiple_of(i * tile, tile), tile)
            bias = dec_bias_ref[:, pl.ds(pl.multiple_of(own_cols + i * tile, tile), tile)]
            rows = arrived[pl.ds(pair_at * group_rows, group_rows), cols]
            error = (
                jnp.dot(low, dec[:, cols], preferred_element_type=jnp.float32)
                + bias
                - rows.astype(jnp.float32)
            )
            squares[:, cols] += jnp.sum(
                (error * error).reshape(group_rows // 8, 8, tile), axis=0
            )
            term = jnp.dot(
                flipped, error.astype(jnp.bfloat16), preferred_element_type=jnp.float32
            )
            if pair_at > 0:
                term = grad_ref[0, :, cols] + term
            if pair_at == len(pairs) - 1:
                term = term / (tok_rows * replicas)
            grad_ref[0, :, cols] = term
            return carry

        lax.fori_loop(0, tiles, step, 0)

    for pair_at in range(len(pairs)):
        encode(pair_at)
        if pair_at > 0:
            decode(pair_at - 1)
    decode(len(pairs) - 1)

    own = squares[:, :128]
    for i in range(1, width // 128):
        own = own + squares[:, i * 128 : (i + 1) * 128]
    place_of = lat * replicas + blk
    losses[place_of] = own
    loss_copies = []
    for j, e in peers:
        copy = pltpu.make_async_remote_copy(
            src_ref=losses.at[place_of],
            dst_ref=losses.at[place_of],
            send_sem=loss_send.at[j * replicas + e],
            recv_sem=loss_recv.at[j * replicas + e],
            device_id=device(j, e),
            device_id_type=MESH,
        )
        copy.start()
        loss_copies.append(copy)

    for j, copy in code_copies:
        if j == 0:
            copy.wait()
        else:
            copy.wait_recv()
    codes_out_ref[...] = jnp.dot(
        to_token.astype(jnp.bfloat16), returned[...], preferred_element_type=jnp.float32
    ).astype(jnp.bfloat16)

    for copy in loss_copies:
        copy.wait_recv()
    total = jnp.sum(losses[...], axis=0)
    loss_ref[...] = jnp.sum(total, keepdims=True) / (
        tok_rows * groups * replicas * features
    )

    for j, e in peers:
        row_copies[j, e].wait_send()
    for copy in part_copies + loss_copies:
        copy.wait_send()
    for j, copy in code_copies:
        if j > 0:
            copy.wait_send()


def routed(activations, block_ids, enc_weight, enc_bias, dec_weight, dec_bias):
    groups = lax.axis_size("latent")
    replicas = lax.axis_size("blk")
    devices = groups * replicas
    tok_rows, features = activations.shape
    latents = enc_weight.shape[2]
    seg = tok_rows // groups
    width = features // replicas
    pairs = groups // 2
    tile = min(512, width)
    vmem = pl.BlockSpec(memory_space=pltpu.VMEM)
    hbm = pl.BlockSpec(memory_space=pl.ANY)
    dma = pltpu.SemaphoreType.DMA
    loss, codes, gradient = pl.pallas_call(
        functools.partial(kernel, groups, replicas, tile),
        out_shape=(
            jax.ShapeDtypeStruct((1, 1), jnp.float32),
            jax.ShapeDtypeStruct((tok_rows, latents), jnp.bfloat16),
            jax.ShapeDtypeStruct((1, latents, width), jnp.float32),
        ),
        in_specs=[vmem, vmem, vmem, hbm, hbm, hbm],
        out_specs=(vmem, vmem, vmem),
        scratch_shapes=[
            pltpu.VMEM((tok_rows, features), jnp.bfloat16),
            pltpu.VMEM((tok_rows, features), jnp.bfloat16),
            pltpu.VMEM((devices * seg, width), jnp.bfloat16),
            pltpu.VMEM((width, latents), jnp.bfloat16),
            pltpu.VMEM((latents, width), jnp.bfloat16),
            pltpu.VMEM((pairs, replicas, 2 * replicas * seg, latents), jnp.float32),
            pltpu.VMEM((devices * seg, latents), jnp.bfloat16),
            pltpu.VMEM((tok_rows, latents), jnp.bfloat16),
            pltpu.VMEM((8, width), jnp.float32),
            pltpu.VMEM((devices, 8, 128), jnp.float32),
            dma((replicas + 2,)),
            dma((devices,)),
            dma((devices,)),
            dma((pairs * replicas,)),
            dma((pairs * replicas,)),
            dma((groups,)),
            dma((groups,)),
            dma((devices,)),
            dma((devices,)),
        ],
        compiler_params=pltpu.CompilerParams(
            collective_id=0, has_side_effects=True, vmem_limit_bytes=40 * 1024 * 1024
        ),
    )(
        block_ids,
        enc_bias,
        dec_bias.reshape(1, features),
        activations,
        enc_weight,
        dec_weight,
    )
    return loss[0, 0], codes, gradient


def spread(activations, block_ids, enc_weight, enc_bias, dec_weight, dec_bias):
    groups = lax.axis_size("latent")
    replicas = lax.axis_size("blk")
    tok_rows, features = activations.shape
    per_owner = tok_rows // groups
    block_of = block_ids[:, 0]
    matches = (block_of[:, None] == block_of[None, :]).astype(jnp.int32)
    earlier = jnp.sum(jnp.tril(matches, -1), axis=1)
    placed = block_of * per_owner + earlier
    source_row = (
        jnp.zeros((tok_rows,), jnp.int32).at[placed].set(jnp.arange(tok_rows, dtype=jnp.int32))
    )
    outgoing = activations[source_row]
    contract = (((0,), (0,)), ((), ()))
    incoming = lax.all_to_all(outgoing, "latent", split_axis=0, concat_axis=0, tiled=True)
    centered = (incoming.astype(jnp.float32) - dec_bias).astype(jnp.bfloat16)
    pre_codes = jnp.dot(centered, enc_weight[0], preferred_element_type=jnp.float32) + enc_bias[0]
    codes = jnp.maximum(pre_codes, 0.0).astype(jnp.bfloat16)
    error_rows = (
        jnp.dot(codes, dec_weight[0], preferred_element_type=jnp.float32)
        + dec_bias
        - incoming.astype(jnp.float32)
    )
    squares = jnp.sum(error_rows * error_rows)
    partial_grad = lax.dot_general(
        codes, error_rows.astype(jnp.bfloat16), contract, preferred_element_type=jnp.float32
    )
    summed = lax.psum_scatter(
        partial_grad.astype(jnp.bfloat16), "blk", scatter_dimension=1, tiled=True
    ).astype(jnp.float32)
    returned = lax.all_to_all(codes, "latent", split_axis=0, concat_axis=0, tiled=True)
    token_codes = returned[placed]
    gradient = summed / (tok_rows * replicas)
    summed_loss = lax.psum(squares, ("latent", "blk"))
    loss_value = summed_loss / (tok_rows * groups * replicas * features)
    return (loss_value, token_codes, gradient[None])


def solution(mesh):
    groups, replicas = mesh.shape["latent"], mesh.shape["blk"]
    placed = (
        P(("latent", "blk"), None),
        P(("latent", "blk"), None),
        P("latent", None, None),
        P("latent", None),
        P("latent", None, None),
        P(),
    )

    def local(activations, *rest):
        tok_rows, features = activations.shape
        fits = (
            groups & (groups - 1) == 0
            and replicas & (replicas - 1) == 0
            and tok_rows % (16 * groups) == 0
            and features % (128 * replicas) == 0
        )
        return (routed if fits else spread)(activations, *rest)

    return jax.shard_map(
        local,
        mesh=mesh,
        in_specs=placed,
        out_specs=(P(), P(("latent", "blk"), None), P("latent", None, "blk")),
        check_vma=False,
    )
```

```python
import functools
import math

import jax
import jax.numpy as jnp
from jax import lax
from jax.experimental import pallas as pl
from jax.experimental.pallas import tpu as pltpu
from jax.sharding import PartitionSpec as P

MESH = pl.DeviceIdType.MESH


def flip(index, mask):
    out, bit = index, 1
    while bit <= mask:
        if mask & bit:
            out = out + bit * (1 - 2 * ((index // bit) % 2))
        bit *= 2
    return out


def kernel(
    groups,
    replicas,
    tile,
    ids_ref,
    enc_bias_ref,
    dec_bias_ref,
    act_hbm,
    enc_hbm,
    dec_hbm,
    loss_ref,
    codes_out_ref,
    grad_hbm,
    act,
    ordered,
    arrived,
    enc,
    dec,
    parts,
    codes,
    returned,
    squares,
    losses,
    error_low,
    grad,
    load_sem,
    row_send,
    row_recv,
    part_send,
    part_recv,
    code_send,
    code_recv,
    loss_send,
    loss_recv,
):
    lat, blk = lax.axis_index("latent"), lax.axis_index("blk")
    tok_rows, features = act.shape
    seg = tok_rows // groups
    width = features // replicas
    latents = enc.shape[1]
    tiles = width // tile
    group_rows = replicas * seg
    own_cols = pl.multiple_of(blk * width, width)
    order = [j for i in range(groups // 2) for j in (groups // 2 - 1 - i, groups // 2 + i)]
    ahead = min(4, groups)
    peers = [(j, e) for j in range(groups) for e in range(replicas) if (j, e) != (0, 0)]

    def device(j, e):
        return (flip(lat, j), flip(blk, e))

    barrier = pltpu.get_barrier_semaphore()
    loads = []
    for e in range(replicas):
        cols = pl.ds(pl.multiple_of(flip(blk, e) * width, width), width)
        loads.append(
            pltpu.make_async_copy(act_hbm.at[:, cols], act.at[:, cols], load_sem.at[e])
        )
    load_enc = pltpu.make_async_copy(
        enc_hbm.at[0, pl.ds(own_cols, width), :], enc, load_sem.at[replicas]
    )
    load_dec = pltpu.make_async_copy(
        dec_hbm.at[0, :, pl.ds(own_cols, width)], dec, load_sem.at[replicas + 1]
    )
    for load in loads:
        load.start()
    for j, e in peers:
        pl.semaphore_signal(barrier, inc=1, device_id=device(j, e), device_id_type=MESH)
    load_enc.start()
    load_dec.start()

    ids = ids_ref[...]
    square = (tok_rows, tok_rows)
    down = lax.broadcasted_iota(jnp.int32, square, 0)
    along = lax.broadcasted_iota(jnp.int32, square, 1)
    named = (ids == down).astype(jnp.float32)
    earlier = jnp.dot(
        named.astype(jnp.bfloat16),
        (down < along).astype(jnp.float32).astype(jnp.bfloat16),
        preferred_element_type=jnp.float32,
    )
    place = jnp.sum(named * earlier, axis=0, keepdims=True) + ids.astype(jnp.float32) * seg
    placed = (place == down.astype(jnp.float32)).astype(jnp.float32)
    to_place = placed.astype(jnp.bfloat16)

    row_copies = {}

    def send_rows(at, e):
        j = order[at]
        owner, column = device(j, e)
        source = ordered.at[
            pl.ds(pl.multiple_of(owner * seg, seg), seg),
            pl.ds(pl.multiple_of(column * width, width), width),
        ]
        target = arrived.at[pl.ds(pl.multiple_of((at * replicas + blk) * seg, seg), seg), :]
        if (j, e) == (0, 0):
            copy = pltpu.make_async_copy(source, target, row_recv.at[0])
        else:
            copy = pltpu.make_async_remote_copy(
                src_ref=source,
                dst_ref=target,
                send_sem=row_send.at[j * replicas + e],
                recv_sem=row_recv.at[j * replicas + e],
                device_id=(owner, column),
                device_id_type=MESH,
            )
        copy.start()
        row_copies[j, e] = copy

    def wait_sent(at):
        for e in range(replicas):
            if (order[at], e) != (0, 0):
                row_copies[order[at], e].wait_send()

    for e in range(replicas):
        loads[e].wait()

        def order_rows(i, carry):
            cols = pl.ds(pl.multiple_of(flip(blk, e) * width + i * tile, tile), tile)
            ordered[:, cols] = jnp.dot(
                to_place, act[:, cols], preferred_element_type=jnp.float32
            ).astype(jnp.bfloat16)
            return carry

        lax.fori_loop(0, tiles, order_rows, 0)
        if e == 0:
            pl.semaphore_wait(barrier, len(peers))
        for at in range(ahead):
            send_rows(at, e)

    load_enc.wait()
    load_dec.wait()
    squares[...] = jnp.zeros_like(squares)
    part_copies, code_copies = [], []

    def encode(at):
        for e in range(replicas):
            if (order[at], e) == (0, 0):
                row_copies[0, 0].wait()
            else:
                row_copies[order[at], e].wait_recv()

        def step(i, total):
            cols = pl.ds(pl.multiple_of(i * tile, tile), tile)
            bias = dec_bias_ref[:, pl.ds(pl.multiple_of(own_cols + i * tile, tile), tile)]
            rows = arrived[pl.ds(at * group_rows, group_rows), cols]
            centered = (rows.astype(jnp.float32) - bias).astype(jnp.bfloat16)
            return total + jnp.dot(centered, enc[cols, :], preferred_element_type=jnp.float32)

        parts[at, blk] = lax.fori_loop(
            0, tiles, step, jnp.zeros((group_rows, latents), jnp.float32)
        )
        for e in range(1, replicas):
            copy = pltpu.make_async_remote_copy(
                src_ref=parts.at[at, blk],
                dst_ref=parts.at[at, blk],
                send_sem=part_send.at[at * replicas + e],
                recv_sem=part_recv.at[at * replicas + e],
                device_id=device(0, e),
                device_id_type=MESH,
            )
            copy.start()
            part_copies.append(copy)

    def decode(at):
        for copy in part_copies[at * (replicas - 1) : (at + 1) * (replicas - 1)]:
            copy.wait_recv()
        total = parts[at, 0]
        for d in range(1, replicas):
            total = total + parts[at, d]
        wide = jnp.maximum(total + enc_bias_ref[...], 0.0)
        low = wide.astype(jnp.bfloat16)
        flipped = low.astype(jnp.float32).T.astype(jnp.bfloat16)
        codes[pl.ds(at * group_rows, group_rows), :] = low
        j = order[at]
        home = pl.ds(pl.multiple_of(lat * seg, seg), seg)
        source = codes.at[pl.ds(pl.multiple_of((at * replicas + blk) * seg, seg), seg), :]
        if j == 0:
            copy = pltpu.make_async_copy(source, returned.at[home, :], code_recv.at[0])
        else:
            copy = pltpu.make_async_remote_copy(
                src_ref=source,
                dst_ref=returned.at[home, :],
                send_sem=code_send.at[j],
                recv_sem=code_recv.at[j],
                device_id=device(j, 0),
                device_id_type=MESH,
            )
        copy.start()
        code_copies.append((j, copy))

        def errors(i, carry):
            cols = pl.ds(pl.multiple_of(i * tile, tile), tile)
            bias = dec_bias_ref[:, pl.ds(pl.multiple_of(own_cols + i * tile, tile), tile)]
            rows = arrived[pl.ds(at * group_rows, group_rows), cols]
            error = (
                jnp.dot(low, dec[:, cols], preferred_element_type=jnp.float32)
                + bias
                - rows.astype(jnp.float32)
            )
            squares[:, cols] += jnp.sum(
                (error * error).reshape(group_rows // 8, 8, tile), axis=0
            )
            error_low[:, cols] = error.astype(jnp.bfloat16)
            return carry

        def gradient(i, carry):
            cols = pl.ds(pl.multiple_of(i * tile, tile), tile)
            term = jnp.dot(flipped, error_low[:, cols], preferred_element_type=jnp.float32)
            if at > 0:
                term = grad[:, cols] + term
            if at == groups - 1:
                term = term / (tok_rows * replicas)
            grad[:, cols] = term
            return carry

        lax.fori_loop(0, tiles, errors, 0)
        if at == groups - 1:
            send_squares()
        lax.fori_loop(0, tiles, gradient, 0)

    place_of = lat * replicas + blk
    loss_copies = []

    def send_squares():
        own = squares[:, :128]
        for i in range(1, width // 128):
            own = own + squares[:, i * 128 : (i + 1) * 128]
        losses[place_of] = own
        for j, e in peers:
            copy = pltpu.make_async_remote_copy(
                src_ref=losses.at[place_of],
                dst_ref=losses.at[place_of],
                send_sem=loss_send.at[j * replicas + e],
                recv_sem=loss_recv.at[j * replicas + e],
                device_id=device(j, e),
                device_id_type=MESH,
            )
            copy.start()
            loss_copies.append(copy)

    for at in range(groups):
        if at + ahead < groups:
            wait_sent(at)
            for e in range(replicas):
                send_rows(at + ahead, e)
        encode(at)
        if at > 0:
            decode(at - 1)
    decode(groups - 1)
    store = pltpu.make_async_copy(grad, grad_hbm.at[0], load_sem.at[0])
    store.start()

    for j, copy in code_copies:
        if j == 0:
            copy.wait()
        else:
            copy.wait_recv()
    codes_out_ref[...] = jnp.dot(
        placed.T.astype(jnp.bfloat16), returned[...], preferred_element_type=jnp.float32
    ).astype(jnp.bfloat16)

    for copy in loss_copies:
        copy.wait_recv()
    total = jnp.sum(losses[...], axis=0)
    loss_ref[...] = jnp.sum(total, keepdims=True) / (
        tok_rows * groups * replicas * features
    )

    store.wait()
    for at in range(groups - ahead, groups):
        wait_sent(at)
    for copy in part_copies + loss_copies:
        copy.wait_send()
    for j, copy in code_copies:
        if j > 0:
            copy.wait_send()


def routed(activations, block_ids, enc_weight, enc_bias, dec_weight, dec_bias):
    groups = lax.axis_size("latent")
    replicas = lax.axis_size("blk")
    devices = groups * replicas
    tok_rows, features = activations.shape
    latents = enc_weight.shape[2]
    seg = tok_rows // groups
    width = features // replicas
    tile = math.gcd(512, width)
    vmem = pl.BlockSpec(memory_space=pltpu.VMEM)
    hbm = pl.BlockSpec(memory_space=pl.ANY)
    dma = pltpu.SemaphoreType.DMA
    loss, codes, gradient = pl.pallas_call(
        functools.partial(kernel, groups, replicas, tile),
        out_shape=(
            jax.ShapeDtypeStruct((1, 1), jnp.float32),
            jax.ShapeDtypeStruct((tok_rows, latents), jnp.bfloat16),
            jax.ShapeDtypeStruct((1, latents, width), jnp.float32),
        ),
        in_specs=[vmem, vmem, vmem, hbm, hbm, hbm],
        out_specs=(vmem, vmem, hbm),
        scratch_shapes=[
            pltpu.VMEM((tok_rows, features), jnp.bfloat16),
            pltpu.VMEM((tok_rows, features), jnp.bfloat16),
            pltpu.VMEM((devices * seg, width), jnp.bfloat16),
            pltpu.VMEM((width, latents), jnp.bfloat16),
            pltpu.VMEM((latents, width), jnp.bfloat16),
            pltpu.VMEM((groups, replicas, replicas * seg, latents), jnp.float32),
            pltpu.VMEM((devices * seg, latents), jnp.bfloat16),
            pltpu.VMEM((tok_rows, latents), jnp.bfloat16),
            pltpu.VMEM((8, width), jnp.float32),
            pltpu.VMEM((devices, 8, 128), jnp.float32),
            pltpu.VMEM((replicas * seg, width), jnp.bfloat16),
            pltpu.VMEM((latents, width), jnp.float32),
            dma((replicas + 2,)),
            dma((devices,)),
            dma((devices,)),
            dma((devices,)),
            dma((devices,)),
            dma((groups,)),
            dma((groups,)),
            dma((devices,)),
            dma((devices,)),
        ],
        compiler_params=pltpu.CompilerParams(
            collective_id=0, has_side_effects=True, vmem_limit_bytes=60 * 1024 * 1024
        ),
    )(
        block_ids.reshape(1, tok_rows),
        enc_bias,
        dec_bias.reshape(1, features),
        activations,
        enc_weight,
        dec_weight,
    )
    return loss[0, 0], codes, gradient


def spread(activations, block_ids, enc_weight, enc_bias, dec_weight, dec_bias):
    groups = lax.axis_size("latent")
    replicas = lax.axis_size("blk")
    tok_rows, features = activations.shape
    per_owner = tok_rows // groups
    block_of = block_ids[:, 0]
    matches = (block_of[:, None] == block_of[None, :]).astype(jnp.int32)
    earlier = jnp.sum(jnp.tril(matches, -1), axis=1)
    placed = block_of * per_owner + earlier
    source_row = (
        jnp.zeros((tok_rows,), jnp.int32).at[placed].set(jnp.arange(tok_rows, dtype=jnp.int32))
    )
    outgoing = activations[source_row]
    contract = (((0,), (0,)), ((), ()))
    incoming = lax.all_to_all(outgoing, "latent", split_axis=0, concat_axis=0, tiled=True)
    centered = (incoming.astype(jnp.float32) - dec_bias).astype(jnp.bfloat16)
    pre_codes = jnp.dot(centered, enc_weight[0], preferred_element_type=jnp.float32) + enc_bias[0]
    codes = jnp.maximum(pre_codes, 0.0).astype(jnp.bfloat16)
    error_rows = (
        jnp.dot(codes, dec_weight[0], preferred_element_type=jnp.float32)
        + dec_bias
        - incoming.astype(jnp.float32)
    )
    squares = jnp.sum(error_rows * error_rows)
    partial_grad = lax.dot_general(
        codes, error_rows.astype(jnp.bfloat16), contract, preferred_element_type=jnp.float32
    )
    summed = lax.psum_scatter(
        partial_grad.astype(jnp.bfloat16), "blk", scatter_dimension=1, tiled=True
    ).astype(jnp.float32)
    returned = lax.all_to_all(codes, "latent", split_axis=0, concat_axis=0, tiled=True)
    token_codes = returned[placed]
    gradient = summed / (tok_rows * replicas)
    summed_loss = lax.psum(squares, ("latent", "blk"))
    loss_value = summed_loss / (tok_rows * groups * replicas * features)
    return (loss_value, token_codes, gradient[None])


def solution(mesh):
    groups, replicas = mesh.shape["latent"], mesh.shape["blk"]
    placed = (
        P(("latent", "blk"), None),
        P(("latent", "blk"), None),
        P("latent", None, None),
        P("latent", None),
        P("latent", None, None),
        P(),
    )

    def local(activations, *rest):
        tok_rows, features = activations.shape
        fits = (
            groups & (groups - 1) == 0
            and replicas & (replicas - 1) == 0
            and 1 < groups <= tok_rows
            and tok_rows % (16 * groups) == 0
            and features % (128 * replicas) == 0
        )
        return (routed if fits else spread)(activations, *rest)

    return jax.shard_map(
        local,
        mesh=mesh,
        in_specs=placed,
        out_specs=(P(), P(("latent", "blk"), None), P("latent", None, "blk")),
        check_vma=False,
    )
```

```python
import functools
import math

import jax
import jax.numpy as jnp
from jax import lax
from jax.experimental import pallas as pl
from jax.experimental.pallas import tpu as pltpu
from jax.sharding import PartitionSpec as P

MESH = pl.DeviceIdType.MESH


def flip(index, mask):
    out, bit = index, 1
    while bit <= mask:
        if mask & bit:
            out = out + bit * (1 - 2 * ((index // bit) % 2))
        bit *= 2
    return out


def kernel(
    groups,
    replicas,
    tile,
    ids_hbm,
    enc_bias_hbm,
    dec_bias_hbm,
    act_hbm,
    enc_hbm,
    dec_hbm,
    loss_ref,
    codes_out_ref,
    grad_ref,
    ids_ref,
    enc_bias_ref,
    dec_bias_ref,
    act,
    ordered,
    arrived,
    enc,
    dec,
    parts,
    codes,
    returned,
    squares,
    level_losses,
    losses,
    error_low,
    load_sem,
    row_send,
    row_recv,
    part_send,
    part_recv,
    code_send,
    code_recv,
    loss_send,
    loss_recv,
    total_send,
    total_recv,
):
    lat, blk = lax.axis_index("latent"), lax.axis_index("blk")
    tok_rows, features = act.shape
    seg = tok_rows // groups
    width = features // replicas
    latents = enc.shape[1]
    tiles = width // tile
    group_rows = replicas * seg
    own_cols = pl.multiple_of(blk * width, width)
    order = [j for i in range(groups // 2) for j in (groups // 2 - 1 - i, groups // 2 + i)]
    ahead = min(4, groups)
    peers = [(j, e) for j in range(groups) for e in range(replicas) if (j, e) != (0, 0)]

    def device(j, e):
        return (flip(lat, j), flip(blk, e))

    barrier = pltpu.get_barrier_semaphore()
    load_ids = pltpu.make_async_copy(ids_hbm, ids_ref, load_sem.at[replicas + 2])
    load_ids.start()
    loads = []
    for e in range(replicas):
        cols = pl.ds(pl.multiple_of(flip(blk, e) * width, width), width)
        loads.append(
            pltpu.make_async_copy(act_hbm.at[:, cols], act.at[:, cols], load_sem.at[e])
        )
    load_enc = pltpu.make_async_copy(
        enc_hbm.at[0, pl.ds(own_cols, width), :], enc, load_sem.at[replicas]
    )
    load_dec = pltpu.make_async_copy(
        dec_hbm.at[0, :, pl.ds(own_cols, width)], dec, load_sem.at[replicas + 1]
    )
    load_biases = [
        pltpu.make_async_copy(enc_bias_hbm, enc_bias_ref, load_sem.at[replicas + 3]),
        pltpu.make_async_copy(dec_bias_hbm, dec_bias_ref, load_sem.at[replicas + 4]),
    ]
    for load in loads:
        load.start()
    for j, e in reversed(peers):
        pl.semaphore_signal(barrier, inc=1, device_id=device(j, e), device_id_type=MESH)
    for load in (load_enc, load_dec, *load_biases):
        load.start()
    load_ids.wait()

    ids = ids_ref[...]
    square = (tok_rows, tok_rows)
    down = lax.broadcasted_iota(jnp.int32, square, 0)
    along = lax.broadcasted_iota(jnp.int32, square, 1)
    named = (ids == down).astype(jnp.float32)
    earlier = jnp.dot(
        named.astype(jnp.bfloat16),
        (down < along).astype(jnp.float32).astype(jnp.bfloat16),
        preferred_element_type=jnp.float32,
    )
    place = jnp.sum(named * earlier, axis=0, keepdims=True) + ids.astype(jnp.float32) * seg
    placed = (place == down.astype(jnp.float32)).astype(jnp.float32)
    to_place = placed.astype(jnp.bfloat16)

    row_copies = {}

    def send_rows(at, e):
        j = order[at]
        owner, column = device(j, e)
        source = ordered.at[
            pl.ds(pl.multiple_of(owner * seg, seg), seg),
            pl.ds(pl.multiple_of(column * width, width), width),
        ]
        target = arrived.at[pl.ds(pl.multiple_of((at * replicas + blk) * seg, seg), seg), :]
        if (j, e) == (0, 0):
            copy = pltpu.make_async_copy(source, target, row_recv.at[0])
        else:
            copy = pltpu.make_async_remote_copy(
                src_ref=source,
                dst_ref=target,
                send_sem=row_send.at[j * replicas + e],
                recv_sem=row_recv.at[j * replicas + e],
                device_id=(owner, column),
                device_id_type=MESH,
            )
        copy.start()
        row_copies[j, e] = copy

    def wait_sent(at):
        for e in range(replicas):
            if (order[at], e) != (0, 0):
                row_copies[order[at], e].wait_send()

    for e in range(replicas):
        loads[e].wait()

        def order_rows(i, carry):
            cols = pl.ds(pl.multiple_of(flip(blk, e) * width + i * tile, tile), tile)
            ordered[:, cols] = jnp.dot(
                to_place, act[:, cols], preferred_element_type=jnp.float32
            ).astype(jnp.bfloat16)
            return carry

        lax.fori_loop(0, tiles, order_rows, 0)
        if e == 0:
            pl.semaphore_wait(barrier, len(peers))
        for at in range(ahead):
            send_rows(at, e)

    for at in range(ahead, groups):
        for e in range(replicas):
            send_rows(at, e)

    for load in (load_enc, load_dec, *load_biases):
        load.wait()
    squares[...] = jnp.zeros_like(squares)
    part_copies, code_copies = [], []

    def encode(at):
        for e in range(replicas):
            if (order[at], e) == (0, 0):
                row_copies[0, 0].wait()
            else:
                row_copies[order[at], e].wait_recv()

        def step(i, total):
            cols = pl.ds(pl.multiple_of(i * tile, tile), tile)
            bias = dec_bias_ref[:, pl.ds(pl.multiple_of(own_cols + i * tile, tile), tile)]
            rows = arrived[pl.ds(at * group_rows, group_rows), cols]
            centered = (rows.astype(jnp.float32) - bias).astype(jnp.bfloat16)
            return total + jnp.dot(centered, enc[cols, :], preferred_element_type=jnp.float32)

        parts[at, blk] = lax.fori_loop(
            0, tiles, step, jnp.zeros((group_rows, latents), jnp.float32)
        )
        for e in range(1, replicas):
            copy = pltpu.make_async_remote_copy(
                src_ref=parts.at[at, blk],
                dst_ref=parts.at[at, blk],
                send_sem=part_send.at[at * replicas + e],
                recv_sem=part_recv.at[at * replicas + e],
                device_id=device(0, e),
                device_id_type=MESH,
            )
            copy.start()
            part_copies.append(copy)

    def decode(at):
        for copy in part_copies[at * (replicas - 1) : (at + 1) * (replicas - 1)]:
            copy.wait_recv()
        total = parts[at, 0]
        for d in range(1, replicas):
            total = total + parts[at, d]
        wide = jnp.maximum(total + enc_bias_ref[...], 0.0)
        low = wide.astype(jnp.bfloat16)
        flipped = low.astype(jnp.float32).T.astype(jnp.bfloat16)
        codes[pl.ds(at * group_rows, group_rows), :] = low
        j = order[at]
        home = pl.ds(pl.multiple_of(lat * seg, seg), seg)
        source = codes.at[pl.ds(pl.multiple_of((at * replicas + blk) * seg, seg), seg), :]
        if j == 0:
            copy = pltpu.make_async_copy(source, returned.at[home, :], code_recv.at[0])
        else:
            copy = pltpu.make_async_remote_copy(
                src_ref=source,
                dst_ref=returned.at[home, :],
                send_sem=code_send.at[j],
                recv_sem=code_recv.at[j],
                device_id=device(j, 0),
                device_id_type=MESH,
            )
        copy.start()
        code_copies.append((j, copy))

        def errors(i, carry):
            cols = pl.ds(pl.multiple_of(i * tile, tile), tile)
            bias = dec_bias_ref[:, pl.ds(pl.multiple_of(own_cols + i * tile, tile), tile)]
            rows = arrived[pl.ds(at * group_rows, group_rows), cols]
            error = (
                jnp.dot(low, dec[:, cols], preferred_element_type=jnp.float32)
                + bias
                - rows.astype(jnp.float32)
            )
            squares[:, cols] += jnp.sum(
                (error * error).reshape(group_rows // 8, 8, tile), axis=0
            )
            error_low[:, cols] = error.astype(jnp.bfloat16)
            return carry

        def gradient(i, carry):
            cols = pl.ds(pl.multiple_of(i * tile, tile), tile)
            term = jnp.dot(flipped, error_low[:, cols], preferred_element_type=jnp.float32)
            if at > 0:
                term = grad_ref[0, :, cols] + term
            if at == groups - 1:
                term = term / (tok_rows * replicas)
            grad_ref[0, :, cols] = term
            return carry

        lax.fori_loop(0, tiles, errors, 0)
        if at == groups - 1:
            send_squares()
        lax.fori_loop(0, tiles, gradient, 0)

    loss_copies, total_copies = [], []

    def send_squares():
        own = squares[:, :128]
        for i in range(1, width // 128):
            own = own + squares[:, i * 128 : (i + 1) * 128]
        level_losses[lat] = own
        for j in range(groups - 1, 0, -1):
            copy = pltpu.make_async_remote_copy(
                src_ref=level_losses.at[lat],
                dst_ref=level_losses.at[lat],
                send_sem=loss_send.at[j],
                recv_sem=loss_recv.at[j],
                device_id=device(j, 0),
                device_id_type=MESH,
            )
            copy.start()
            loss_copies.append(copy)

    for at in range(groups):
        encode(at)
        if at > 0:
            decode(at - 1)
    decode(groups - 1)
    for copy in loss_copies:
        copy.wait_recv()
    losses[blk] = jnp.sum(level_losses[...], axis=0)
    for e in range(replicas - 1, 0, -1):
        copy = pltpu.make_async_remote_copy(
            src_ref=losses.at[blk],
            dst_ref=losses.at[blk],
            send_sem=total_send.at[e],
            recv_sem=total_recv.at[e],
            device_id=device(0, e),
            device_id_type=MESH,
        )
        copy.start()
        total_copies.append(copy)

    for j, copy in code_copies:
        if j == 0:
            copy.wait()
        else:
            copy.wait_recv()
    codes_out_ref[...] = jnp.dot(
        placed.T.astype(jnp.bfloat16), returned[...], preferred_element_type=jnp.float32
    ).astype(jnp.bfloat16)

    for copy in total_copies:
        copy.wait_recv()
    total = jnp.sum(losses[...], axis=0)
    loss_ref[...] = jnp.sum(total, keepdims=True) / (
        tok_rows * groups * replicas * features
    )

    for at in range(groups):
        wait_sent(at)
    for copy in part_copies + loss_copies + total_copies:
        copy.wait_send()
    for j, copy in code_copies:
        if j > 0:
            copy.wait_send()


def routed(activations, block_ids, enc_weight, enc_bias, dec_weight, dec_bias):
    groups = lax.axis_size("latent")
    replicas = lax.axis_size("blk")
    devices = groups * replicas
    tok_rows, features = activations.shape
    latents = enc_weight.shape[2]
    seg = tok_rows // groups
    width = features // replicas
    tile = math.gcd(512, width)
    vmem = pl.BlockSpec(memory_space=pltpu.VMEM)
    hbm = pl.BlockSpec(memory_space=pltpu.HBM)
    dma = pltpu.SemaphoreType.DMA
    loss, codes, gradient = pl.pallas_call(
        functools.partial(kernel, groups, replicas, tile),
        out_shape=(
            jax.ShapeDtypeStruct((1, 1), jnp.float32),
            jax.ShapeDtypeStruct((tok_rows, latents), jnp.bfloat16),
            jax.ShapeDtypeStruct((1, latents, width), jnp.float32),
        ),
        in_specs=[hbm] * 6,
        out_specs=(vmem, vmem, vmem),
        scratch_shapes=[
            pltpu.VMEM((1, tok_rows), jnp.int32),
            pltpu.VMEM((1, latents), jnp.float32),
            pltpu.VMEM((1, features), jnp.float32),
            pltpu.VMEM((tok_rows, features), jnp.bfloat16),
            pltpu.VMEM((tok_rows, features), jnp.bfloat16),
            pltpu.VMEM((devices * seg, width), jnp.bfloat16),
            pltpu.VMEM((width, latents), jnp.bfloat16),
            pltpu.VMEM((latents, width), jnp.bfloat16),
            pltpu.VMEM((groups, replicas, replicas * seg, latents), jnp.float32),
            pltpu.VMEM((devices * seg, latents), jnp.bfloat16),
            pltpu.VMEM((tok_rows, latents), jnp.bfloat16),
            pltpu.VMEM((8, width), jnp.float32),
            pltpu.VMEM((groups, 8, 128), jnp.float32),
            pltpu.VMEM((replicas, 8, 128), jnp.float32),
            pltpu.VMEM((replicas * seg, width), jnp.bfloat16),
            dma((replicas + 5,)),
            dma((devices,)),
            dma((devices,)),
            dma((devices,)),
            dma((devices,)),
            dma((groups,)),
            dma((groups,)),
            dma((groups,)),
            dma((groups,)),
            dma((replicas,)),
            dma((replicas,)),
        ],
        compiler_params=pltpu.CompilerParams(
            collective_id=0, has_side_effects=True, vmem_limit_bytes=52 * 1024 * 1024
        ),
    )(
        block_ids.reshape(1, tok_rows),
        enc_bias,
        dec_bias.reshape(1, features),
        activations,
        enc_weight,
        dec_weight,
    )
    return loss[0, 0], codes, gradient


def spread(activations, block_ids, enc_weight, enc_bias, dec_weight, dec_bias):
    groups = lax.axis_size("latent")
    replicas = lax.axis_size("blk")
    tok_rows, features = activations.shape
    per_owner = tok_rows // groups
    block_of = block_ids[:, 0]
    matches = (block_of[:, None] == block_of[None, :]).astype(jnp.int32)
    earlier = jnp.sum(jnp.tril(matches, -1), axis=1)
    placed = block_of * per_owner + earlier
    source_row = (
        jnp.zeros((tok_rows,), jnp.int32).at[placed].set(jnp.arange(tok_rows, dtype=jnp.int32))
    )
    outgoing = activations[source_row]
    contract = (((0,), (0,)), ((), ()))
    incoming = lax.all_to_all(outgoing, "latent", split_axis=0, concat_axis=0, tiled=True)
    centered = (incoming.astype(jnp.float32) - dec_bias).astype(jnp.bfloat16)
    pre_codes = jnp.dot(centered, enc_weight[0], preferred_element_type=jnp.float32) + enc_bias[0]
    codes = jnp.maximum(pre_codes, 0.0).astype(jnp.bfloat16)
    error_rows = (
        jnp.dot(codes, dec_weight[0], preferred_element_type=jnp.float32)
        + dec_bias
        - incoming.astype(jnp.float32)
    )
    squares = jnp.sum(error_rows * error_rows)
    partial_grad = lax.dot_general(
        codes, error_rows.astype(jnp.bfloat16), contract, preferred_element_type=jnp.float32
    )
    summed = lax.psum_scatter(
        partial_grad.astype(jnp.bfloat16), "blk", scatter_dimension=1, tiled=True
    ).astype(jnp.float32)
    returned = lax.all_to_all(codes, "latent", split_axis=0, concat_axis=0, tiled=True)
    token_codes = returned[placed]
    gradient = summed / (tok_rows * replicas)
    summed_loss = lax.psum(squares, ("latent", "blk"))
    loss_value = summed_loss / (tok_rows * groups * replicas * features)
    return (loss_value, token_codes, gradient[None])


def solution(mesh):
    groups, replicas = mesh.shape["latent"], mesh.shape["blk"]
    placed = (
        P(("latent", "blk"), None),
        P(("latent", "blk"), None),
        P("latent", None, None),
        P("latent", None),
        P("latent", None, None),
        P(),
    )

    def local(activations, *rest):
        tok_rows, features = activations.shape
        fits = (
            groups & (groups - 1) == 0
            and replicas & (replicas - 1) == 0
            and 1 < groups <= tok_rows
            and tok_rows % (16 * groups) == 0
            and features % (128 * replicas) == 0
        )
        return (routed if fits else spread)(activations, *rest)

    return jax.shard_map(
        local,
        mesh=mesh,
        in_specs=placed,
        out_specs=(P(), P(("latent", "blk"), None), P("latent", None, "blk")),
        check_vma=False,
    )
```

```python
import functools
import math

import jax
import jax.numpy as jnp
from jax import lax
from jax.experimental import pallas as pl
from jax.experimental.pallas import tpu as pltpu
from jax.sharding import PartitionSpec as P

MESH = pl.DeviceIdType.MESH


def flip(index, mask):
    out, bit = index, 1
    while bit <= mask:
        if mask & bit:
            out = out + bit * (1 - 2 * ((index // bit) % 2))
        bit *= 2
    return out


def kernel(
    groups,
    replicas,
    tile,
    ids_hbm,
    enc_bias_hbm,
    dec_bias_hbm,
    act_hbm,
    enc_hbm,
    dec_hbm,
    loss_ref,
    codes_out_ref,
    grad_ref,
    ids_ref,
    enc_bias_ref,
    dec_bias_ref,
    act,
    ordered,
    staged,
    arrived,
    enc,
    dec,
    parts,
    codes,
    returned,
    squares,
    level_losses,
    losses,
    error_low,
    load_sem,
    row_send,
    row_recv,
    column_send,
    column_recv,
    part_send,
    part_recv,
    code_send,
    code_recv,
    loss_send,
    loss_recv,
    total_send,
    total_recv,
):
    lat, blk = lax.axis_index("latent"), lax.axis_index("blk")
    tok_rows, features = act.shape
    seg = tok_rows // groups
    width = features // replicas
    latents = enc.shape[1]
    tiles = width // tile
    group_rows = replicas * seg
    own_cols = pl.multiple_of(blk * width, width)
    order = [j for i in range(groups // 2) for j in (groups // 2 - 1 - i, groups // 2 + i)]
    peers = [(j, 0) for j in range(1, groups)] + [(0, e) for e in range(1, replicas)]

    def device(j, e):
        return (flip(lat, j), flip(blk, e))

    barrier = pltpu.get_barrier_semaphore()
    load_ids = pltpu.make_async_copy(ids_hbm, ids_ref, load_sem.at[replicas + 2])
    load_ids.start()
    loads = []
    for e in range(replicas):
        cols = pl.ds(pl.multiple_of(flip(blk, e) * width, width), width)
        loads.append(
            pltpu.make_async_copy(act_hbm.at[:, cols], act.at[:, cols], load_sem.at[e])
        )
    load_enc = pltpu.make_async_copy(
        enc_hbm.at[0, pl.ds(own_cols, width), :], enc, load_sem.at[replicas]
    )
    load_dec = pltpu.make_async_copy(
        dec_hbm.at[0, :, pl.ds(own_cols, width)], dec, load_sem.at[replicas + 1]
    )
    load_biases = [
        pltpu.make_async_copy(enc_bias_hbm, enc_bias_ref, load_sem.at[replicas + 3]),
        pltpu.make_async_copy(dec_bias_hbm, dec_bias_ref, load_sem.at[replicas + 4]),
    ]
    for load in loads:
        load.start()
    for j, e in reversed(peers):
        pl.semaphore_signal(barrier, inc=1, device_id=device(j, e), device_id_type=MESH)
    for load in (load_enc, load_dec, *load_biases):
        load.start()
    load_ids.wait()

    ids = ids_ref[...]
    square = (tok_rows, tok_rows)
    down = lax.broadcasted_iota(jnp.int32, square, 0)
    along = lax.broadcasted_iota(jnp.int32, square, 1)
    named = (ids == down).astype(jnp.float32)
    earlier = jnp.dot(
        named.astype(jnp.bfloat16),
        (down < along).astype(jnp.float32).astype(jnp.bfloat16),
        preferred_element_type=jnp.float32,
    )
    place = jnp.sum(named * earlier, axis=0, keepdims=True) + ids.astype(jnp.float32) * seg
    placed = (place == down.astype(jnp.float32)).astype(jnp.float32)
    to_place = placed.astype(jnp.bfloat16)

    row_copies, column_copies = {}, {}

    def piece(j, e):
        return (
            pl.ds(pl.multiple_of(flip(lat, j) * seg, seg), seg),
            pl.ds(pl.multiple_of(flip(blk, e) * width, width), width),
        )

    def place_at(at, e):
        return pl.ds(pl.multiple_of((at * replicas + flip(blk, e)) * seg, seg), seg)

    def send_rows(at, e):
        j = order[at]
        target = arrived.at[place_at(at, e), :]
        source = ordered.at[piece(j, e)] if e == 0 else staged.at[place_at(at, e), :]
        if j == 0:
            copy = pltpu.make_async_copy(source, target, row_recv.at[0])
        else:
            copy = pltpu.make_async_remote_copy(
                src_ref=source,
                dst_ref=target,
                send_sem=row_send.at[j * replicas + e],
                recv_sem=row_recv.at[j * replicas + e],
                device_id=device(j, 0),
                device_id_type=MESH,
            )
        copy.start()
        row_copies[j, e] = copy

    def send_columns(at, e):
        j = order[at]
        landing = arrived if j == 0 else staged
        copy = pltpu.make_async_remote_copy(
            src_ref=ordered.at[piece(j, e)],
            dst_ref=landing.at[place_at(at, 0), :],
            send_sem=column_send.at[j * replicas + e],
            recv_sem=column_recv.at[j * replicas + e],
            device_id=device(0, e),
            device_id_type=MESH,
        )
        copy.start()
        column_copies[j, e] = copy

    for e in range(replicas):
        loads[e].wait()

        def order_rows(i, carry):
            cols = pl.ds(pl.multiple_of(flip(blk, e) * width + i * tile, tile), tile)
            ordered[:, cols] = jnp.dot(
                to_place, act[:, cols], preferred_element_type=jnp.float32
            ).astype(jnp.bfloat16)
            return carry

        lax.fori_loop(0, tiles, order_rows, 0)
        if e == 0:
            pl.semaphore_wait(barrier, len(peers))
            for at in range(groups):
                send_rows(at, 0)
    for at in range(groups):
        for e in range(1, replicas):
            send_columns(at, e)
    for at in range(groups):
        if order[at] > 0:
            for e in range(1, replicas):
                column_copies[order[at], e].wait_recv()
                send_rows(at, e)

    for load in (load_enc, load_dec, *load_biases):
        load.wait()
    squares[...] = jnp.zeros_like(squares)
    part_copies, code_copies = [], []

    def encode(at):
        for e in range(replicas):
            if (order[at], e) == (0, 0):
                row_copies[0, 0].wait()
            elif order[at] == 0:
                column_copies[0, e].wait_recv()
            else:
                row_copies[order[at], e].wait_recv()

        def step(i, total):
            cols = pl.ds(pl.multiple_of(i * tile, tile), tile)
            bias = dec_bias_ref[:, pl.ds(pl.multiple_of(own_cols + i * tile, tile), tile)]
            rows = arrived[pl.ds(at * group_rows, group_rows), cols]
            centered = (rows.astype(jnp.float32) - bias).astype(jnp.bfloat16)
            return total + jnp.dot(centered, enc[cols, :], preferred_element_type=jnp.float32)

        parts[at, blk] = lax.fori_loop(
            0, tiles, step, jnp.zeros((group_rows, latents), jnp.float32)
        )
        for e in range(1, replicas):
            copy = pltpu.make_async_remote_copy(
                src_ref=parts.at[at, blk],
                dst_ref=parts.at[at, blk],
                send_sem=part_send.at[at * replicas + e],
                recv_sem=part_recv.at[at * replicas + e],
                device_id=device(0, e),
                device_id_type=MESH,
            )
            copy.start()
            part_copies.append(copy)

    def decode(at):
        for copy in part_copies[at * (replicas - 1) : (at + 1) * (replicas - 1)]:
            copy.wait_recv()
        total = parts[at, 0]
        for d in range(1, replicas):
            total = total + parts[at, d]
        wide = jnp.maximum(total + enc_bias_ref[...], 0.0)
        low = wide.astype(jnp.bfloat16)
        flipped = low.astype(jnp.float32).T.astype(jnp.bfloat16)
        codes[pl.ds(at * group_rows, group_rows), :] = low
        j = order[at]
        home = pl.ds(pl.multiple_of(lat * seg, seg), seg)
        source = codes.at[pl.ds(pl.multiple_of((at * replicas + blk) * seg, seg), seg), :]
        if j == 0:
            copy = pltpu.make_async_copy(source, returned.at[home, :], code_recv.at[0])
        else:
            copy = pltpu.make_async_remote_copy(
                src_ref=source,
                dst_ref=returned.at[home, :],
                send_sem=code_send.at[j],
                recv_sem=code_recv.at[j],
                device_id=device(j, 0),
                device_id_type=MESH,
            )
        copy.start()
        code_copies.append((j, copy))

        def errors(i, carry):
            cols = pl.ds(pl.multiple_of(i * tile, tile), tile)
            bias = dec_bias_ref[:, pl.ds(pl.multiple_of(own_cols + i * tile, tile), tile)]
            rows = arrived[pl.ds(at * group_rows, group_rows), cols]
            error = (
                jnp.dot(low, dec[:, cols], preferred_element_type=jnp.float32)
                + bias
                - rows.astype(jnp.float32)
            )
            squares[:, cols] += jnp.sum(
                (error * error).reshape(group_rows // 8, 8, tile), axis=0
            )
            error_low[:, cols] = error.astype(jnp.bfloat16)
            return carry

        def gradient(i, carry):
            cols = pl.ds(pl.multiple_of(i * tile, tile), tile)
            term = jnp.dot(flipped, error_low[:, cols], preferred_element_type=jnp.float32)
            if at > 0:
                term = grad_ref[0, :, cols] + term
            if at == groups - 1:
                term = term / (tok_rows * replicas)
            grad_ref[0, :, cols] = term
            return carry

        lax.fori_loop(0, tiles, errors, 0)
        if at == groups - 1:
            send_squares()
        lax.fori_loop(0, tiles, gradient, 0)

    loss_copies, total_copies = [], []

    def send_squares():
        own = squares[:, :128]
        for i in range(1, width // 128):
            own = own + squares[:, i * 128 : (i + 1) * 128]
        level_losses[lat] = own
        for j in range(groups - 1, 0, -1):
            copy = pltpu.make_async_remote_copy(
                src_ref=level_losses.at[lat],
                dst_ref=level_losses.at[lat],
                send_sem=loss_send.at[j],
                recv_sem=loss_recv.at[j],
                device_id=device(j, 0),
                device_id_type=MESH,
            )
            copy.start()
            loss_copies.append(copy)

    for at in range(groups):
        encode(at)
        if at > 0:
            decode(at - 1)
    decode(groups - 1)
    for copy in loss_copies:
        copy.wait_recv()
    losses[blk] = jnp.sum(level_losses[...], axis=0)
    for e in range(replicas - 1, 0, -1):
        copy = pltpu.make_async_remote_copy(
            src_ref=losses.at[blk],
            dst_ref=losses.at[blk],
            send_sem=total_send.at[e],
            recv_sem=total_recv.at[e],
            device_id=device(0, e),
            device_id_type=MESH,
        )
        copy.start()
        total_copies.append(copy)

    for j, copy in code_copies:
        if j == 0:
            copy.wait()
        else:
            copy.wait_recv()
    codes_out_ref[...] = jnp.dot(
        placed.T.astype(jnp.bfloat16), returned[...], preferred_element_type=jnp.float32
    ).astype(jnp.bfloat16)

    for copy in total_copies:
        copy.wait_recv()
    total = jnp.sum(losses[...], axis=0)
    loss_ref[...] = jnp.sum(total, keepdims=True) / (
        tok_rows * groups * replicas * features
    )

    for (j, e), copy in row_copies.items():
        if j > 0:
            copy.wait_send()
    for copy in column_copies.values():
        copy.wait_send()
    for copy in part_copies + loss_copies + total_copies:
        copy.wait_send()
    for j, copy in code_copies:
        if j > 0:
            copy.wait_send()


def routed(activations, block_ids, enc_weight, enc_bias, dec_weight, dec_bias):
    groups = lax.axis_size("latent")
    replicas = lax.axis_size("blk")
    devices = groups * replicas
    tok_rows, features = activations.shape
    latents = enc_weight.shape[2]
    seg = tok_rows // groups
    width = features // replicas
    tile = math.gcd(512, width)
    vmem = pl.BlockSpec(memory_space=pltpu.VMEM)
    hbm = pl.BlockSpec(memory_space=pltpu.HBM)
    dma = pltpu.SemaphoreType.DMA
    loss, codes, gradient = pl.pallas_call(
        functools.partial(kernel, groups, replicas, tile),
        out_shape=(
            jax.ShapeDtypeStruct((1, 1), jnp.float32),
            jax.ShapeDtypeStruct((tok_rows, latents), jnp.bfloat16),
            jax.ShapeDtypeStruct((1, latents, width), jnp.float32),
        ),
        in_specs=[hbm] * 6,
        out_specs=(vmem, vmem, vmem),
        scratch_shapes=[
            pltpu.VMEM((1, tok_rows), jnp.int32),
            pltpu.VMEM((1, latents), jnp.float32),
            pltpu.VMEM((1, features), jnp.float32),
            pltpu.VMEM((tok_rows, features), jnp.bfloat16),
            pltpu.VMEM((tok_rows, features), jnp.bfloat16),
            pltpu.VMEM((devices * seg, width), jnp.bfloat16),
            pltpu.VMEM((devices * seg, width), jnp.bfloat16),
            pltpu.VMEM((width, latents), jnp.bfloat16),
            pltpu.VMEM((latents, width), jnp.bfloat16),
            pltpu.VMEM((groups, replicas, replicas * seg, latents), jnp.float32),
            pltpu.VMEM((devices * seg, latents), jnp.bfloat16),
            pltpu.VMEM((tok_rows, latents), jnp.bfloat16),
            pltpu.VMEM((8, width), jnp.float32),
            pltpu.VMEM((groups, 8, 128), jnp.float32),
            pltpu.VMEM((replicas, 8, 128), jnp.float32),
            pltpu.VMEM((replicas * seg, width), jnp.bfloat16),
            dma((replicas + 5,)),
            dma((devices,)),
            dma((devices,)),
            dma((devices,)),
            dma((devices,)),
            dma((devices,)),
            dma((devices,)),
            dma((groups,)),
            dma((groups,)),
            dma((groups,)),
            dma((groups,)),
            dma((replicas,)),
            dma((replicas,)),
        ],
        compiler_params=pltpu.CompilerParams(
            collective_id=0, has_side_effects=True, vmem_limit_bytes=52 * 1024 * 1024
        ),
    )(
        block_ids.reshape(1, tok_rows),
        enc_bias,
        dec_bias.reshape(1, features),
        activations,
        enc_weight,
        dec_weight,
    )
    return loss[0, 0], codes, gradient


def spread(activations, block_ids, enc_weight, enc_bias, dec_weight, dec_bias):
    groups = lax.axis_size("latent")
    replicas = lax.axis_size("blk")
    tok_rows, features = activations.shape
    per_owner = tok_rows // groups
    block_of = block_ids[:, 0]
    matches = (block_of[:, None] == block_of[None, :]).astype(jnp.int32)
    earlier = jnp.sum(jnp.tril(matches, -1), axis=1)
    placed = block_of * per_owner + earlier
    source_row = (
        jnp.zeros((tok_rows,), jnp.int32).at[placed].set(jnp.arange(tok_rows, dtype=jnp.int32))
    )
    outgoing = activations[source_row]
    contract = (((0,), (0,)), ((), ()))
    incoming = lax.all_to_all(outgoing, "latent", split_axis=0, concat_axis=0, tiled=True)
    centered = (incoming.astype(jnp.float32) - dec_bias).astype(jnp.bfloat16)
    pre_codes = jnp.dot(centered, enc_weight[0], preferred_element_type=jnp.float32) + enc_bias[0]
    codes = jnp.maximum(pre_codes, 0.0).astype(jnp.bfloat16)
    error_rows = (
        jnp.dot(codes, dec_weight[0], preferred_element_type=jnp.float32)
        + dec_bias
        - incoming.astype(jnp.float32)
    )
    squares = jnp.sum(error_rows * error_rows)
    partial_grad = lax.dot_general(
        codes, error_rows.astype(jnp.bfloat16), contract, preferred_element_type=jnp.float32
    )
    summed = lax.psum_scatter(
        partial_grad.astype(jnp.bfloat16), "blk", scatter_dimension=1, tiled=True
    ).astype(jnp.float32)
    returned = lax.all_to_all(codes, "latent", split_axis=0, concat_axis=0, tiled=True)
    token_codes = returned[placed]
    gradient = summed / (tok_rows * replicas)
    summed_loss = lax.psum(squares, ("latent", "blk"))
    loss_value = summed_loss / (tok_rows * groups * replicas * features)
    return (loss_value, token_codes, gradient[None])


def solution(mesh):
    groups, replicas = mesh.shape["latent"], mesh.shape["blk"]
    placed = (
        P(("latent", "blk"), None),
        P(("latent", "blk"), None),
        P("latent", None, None),
        P("latent", None),
        P("latent", None, None),
        P(),
    )

    def local(activations, *rest):
        tok_rows, features = activations.shape
        fits = (
            groups & (groups - 1) == 0
            and replicas & (replicas - 1) == 0
            and 1 < groups <= tok_rows
            and tok_rows % (16 * groups) == 0
            and features % (128 * replicas) == 0
        )
        return (routed if fits else spread)(activations, *rest)

    return jax.shard_map(
        local,
        mesh=mesh,
        in_specs=placed,
        out_specs=(P(), P(("latent", "blk"), None), P("latent", None, "blk")),
        check_vma=False,
    )
```

```python
import functools
import math

import jax
import jax.numpy as jnp
from jax import lax
from jax.experimental import pallas as pl
from jax.experimental.pallas import tpu as pltpu
from jax.sharding import PartitionSpec as P

MESH = pl.DeviceIdType.MESH


def flip(index, mask):
    out, bit = index, 1
    while bit <= mask:
        if mask & bit:
            out = out + bit * (1 - 2 * ((index // bit) % 2))
        bit *= 2
    return out


def kernel(
    groups,
    replicas,
    tile,
    small_hbm,
    act_hbm,
    enc_hbm,
    dec_hbm,
    loss_ref,
    codes_out_ref,
    grad_ref,
    small,
    act,
    ordered,
    staged,
    arrived,
    enc,
    dec,
    parts,
    codes,
    returned,
    squares,
    level_losses,
    losses,
    error_low,
    load_sem,
    row_send,
    row_recv,
    column_send,
    column_recv,
    part_send,
    part_recv,
    code_send,
    code_recv,
    loss_send,
    loss_recv,
    total_send,
    total_recv,
):
    lat, blk = lax.axis_index("latent"), lax.axis_index("blk")
    tok_rows, features = act.shape
    seg = tok_rows // groups
    width = features // replicas
    latents = enc.shape[1]
    tiles = width // tile
    group_rows = replicas * seg
    own_cols = pl.multiple_of(blk * width, width)
    bias_at = tok_rows + latents + own_cols
    order = [j for i in range(groups // 2) for j in (groups // 2 - 1 - i, groups // 2 + i)]
    ahead, window, lag = min(2, groups), replicas + 2, 3
    peers = [(j, 0) for j in range(1, groups)] + [(0, e) for e in range(1, replicas)]

    def device(j, e):
        return (flip(lat, j), flip(blk, e))

    barrier = pltpu.get_barrier_semaphore()
    load_small = pltpu.make_async_copy(small_hbm, small, load_sem.at[replicas + 2])
    load_small.start()
    loads = []
    for e in range(replicas):
        cols = pl.ds(pl.multiple_of(flip(blk, e) * width, width), width)
        loads.append(
            pltpu.make_async_copy(act_hbm.at[:, cols], act.at[:, cols], load_sem.at[e])
        )
    load_enc = pltpu.make_async_copy(
        enc_hbm.at[0, pl.ds(own_cols, width), :], enc, load_sem.at[replicas]
    )
    load_dec = pltpu.make_async_copy(
        dec_hbm.at[0, :, pl.ds(own_cols, width)], dec, load_sem.at[replicas + 1]
    )
    for load in loads:
        load.start()
    for j, e in reversed(peers):
        pl.semaphore_signal(barrier, inc=1, device_id=device(j, e), device_id_type=MESH)
    load_enc.start()
    load_dec.start()
    load_small.wait()

    ids = small[:, :tok_rows]
    square = (tok_rows, tok_rows)
    down = lax.broadcasted_iota(jnp.int32, square, 0)
    along = lax.broadcasted_iota(jnp.int32, square, 1)
    named = (ids == down.astype(jnp.float32)).astype(jnp.float32)
    earlier = jnp.dot(
        named.astype(jnp.bfloat16),
        (down < along).astype(jnp.float32).astype(jnp.bfloat16),
        preferred_element_type=jnp.float32,
    )
    place = jnp.sum(named * earlier, axis=0, keepdims=True) + ids * seg
    placed = (place == down.astype(jnp.float32)).astype(jnp.float32)
    to_place = placed.astype(jnp.bfloat16)

    row_copies, column_copies = {}, {}

    def piece(j, e):
        return (
            pl.ds(pl.multiple_of(flip(lat, j) * seg, seg), seg),
            pl.ds(pl.multiple_of(flip(blk, e) * width, width), width),
        )

    def place_at(at, e):
        return pl.ds(pl.multiple_of((at * replicas + flip(blk, e)) * seg, seg), seg)

    def send_rows(at, e):
        j = order[at]
        target = arrived.at[place_at(at, e), :]
        source = ordered.at[piece(j, e)] if e == 0 else staged.at[place_at(at, e), :]
        if j == 0:
            copy = pltpu.make_async_copy(source, target, row_recv.at[0])
        else:
            copy = pltpu.make_async_remote_copy(
                src_ref=source,
                dst_ref=target,
                send_sem=row_send.at[j * replicas + e],
                recv_sem=row_recv.at[j * replicas + e],
                device_id=device(j, 0),
                device_id_type=MESH,
            )
        copy.start()
        row_copies[j, e] = copy

    def send_columns(at, e):
        j = order[at]
        landing = arrived if j == 0 else staged
        copy = pltpu.make_async_remote_copy(
            src_ref=ordered.at[piece(j, e)],
            dst_ref=landing.at[place_at(at, 0), :],
            send_sem=column_send.at[j * replicas + e],
            recv_sem=column_recv.at[j * replicas + e],
            device_id=device(0, e),
            device_id_type=MESH,
        )
        copy.start()
        column_copies[j, e] = copy

    for e in range(replicas):
        loads[e].wait()

        def order_rows(i, carry):
            cols = pl.ds(pl.multiple_of(flip(blk, e) * width + i * tile, tile), tile)
            ordered[:, cols] = jnp.dot(
                to_place, act[:, cols], preferred_element_type=jnp.float32
            ).astype(jnp.bfloat16)
            return carry

        lax.fori_loop(0, tiles, order_rows, 0)
        if e == 0:
            pl.semaphore_wait(barrier, len(peers))
            for at in range(ahead):
                send_rows(at, 0)
    for at in range(groups):
        for e in range(1, replicas):
            send_columns(at, e)
    load_enc.wait()
    load_dec.wait()
    squares[...] = jnp.zeros_like(squares)
    part_copies, code_copies = [], []

    def encode(at):
        for e in range(replicas):
            if (order[at], e) == (0, 0):
                row_copies[0, 0].wait()
            elif order[at] == 0:
                column_copies[0, e].wait_recv()
            else:
                row_copies[order[at], e].wait_recv()

        def step(i, total):
            cols = pl.ds(pl.multiple_of(i * tile, tile), tile)
            bias = small[:, pl.ds(pl.multiple_of(bias_at + i * tile, 128), tile)]
            rows = arrived[pl.ds(at * group_rows, group_rows), cols]
            centered = (rows.astype(jnp.float32) - bias).astype(jnp.bfloat16)
            return total + jnp.dot(centered, enc[cols, :], preferred_element_type=jnp.float32)

        parts[at, blk] = lax.fori_loop(
            0, tiles, step, jnp.zeros((group_rows, latents), jnp.float32)
        )
        for e in range(1, replicas):
            copy = pltpu.make_async_remote_copy(
                src_ref=parts.at[at, blk],
                dst_ref=parts.at[at, blk],
                send_sem=part_send.at[at * replicas + e],
                recv_sem=part_recv.at[at * replicas + e],
                device_id=device(0, e),
                device_id_type=MESH,
            )
            copy.start()
            part_copies.append(copy)

    def decode(at):
        for copy in part_copies[at * (replicas - 1) : (at + 1) * (replicas - 1)]:
            copy.wait_recv()
        total = parts[at, 0]
        for d in range(1, replicas):
            total = total + parts[at, d]
        wide = jnp.maximum(total + small[:, tok_rows : tok_rows + latents], 0.0)
        low = wide.astype(jnp.bfloat16)
        flipped = low.astype(jnp.float32).T.astype(jnp.bfloat16)
        codes[pl.ds(at * group_rows, group_rows), :] = low
        j = order[at]
        home = pl.ds(pl.multiple_of(lat * seg, seg), seg)
        source = codes.at[pl.ds(pl.multiple_of((at * replicas + blk) * seg, seg), seg), :]
        if j == 0:
            copy = pltpu.make_async_copy(source, returned.at[home, :], code_recv.at[0])
        else:
            copy = pltpu.make_async_remote_copy(
                src_ref=source,
                dst_ref=returned.at[home, :],
                send_sem=code_send.at[j],
                recv_sem=code_recv.at[j],
                device_id=device(j, 0),
                device_id_type=MESH,
            )
        copy.start()
        code_copies.append((j, copy))

        def errors(i, carry):
            cols = pl.ds(pl.multiple_of(i * tile, tile), tile)
            bias = small[:, pl.ds(pl.multiple_of(bias_at + i * tile, 128), tile)]
            rows = arrived[pl.ds(at * group_rows, group_rows), cols]
            error = (
                jnp.dot(low, dec[:, cols], preferred_element_type=jnp.float32)
                + bias
                - rows.astype(jnp.float32)
            )
            squares[:, cols] += jnp.sum(
                (error * error).reshape(group_rows // 8, 8, tile), axis=0
            )
            error_low[:, cols] = error.astype(jnp.bfloat16)
            return carry

        def gradient(i, carry):
            cols = pl.ds(pl.multiple_of(i * tile, tile), tile)
            term = jnp.dot(flipped, error_low[:, cols], preferred_element_type=jnp.float32)
            if at > 0:
                term = grad_ref[0, :, cols] + term
            if at == groups - 1:
                term = term / (tok_rows * replicas)
            grad_ref[0, :, cols] = term
            return carry

        lax.fori_loop(0, tiles, errors, 0)
        if at == groups - 1:
            send_squares()
        lax.fori_loop(0, tiles, gradient, 0)

    loss_copies, total_copies = [], []

    def send_squares():
        own = squares[:, :128]
        for i in range(1, width // 128):
            own = own + squares[:, i * 128 : (i + 1) * 128]
        level_losses[lat] = own
        for j in range(groups - 1, 0, -1):
            copy = pltpu.make_async_remote_copy(
                src_ref=level_losses.at[lat],
                dst_ref=level_losses.at[lat],
                send_sem=loss_send.at[j],
                recv_sem=loss_recv.at[j],
                device_id=device(j, 0),
                device_id_type=MESH,
            )
            copy.start()
            loss_copies.append(copy)

    far, sent = [], set()
    for at in range(groups + lag):
        if at < groups:
            for e in range(replicas):
                j = order[at]
                if j >= groups // 2:
                    if len(far) >= window:
                        row_copies[far[-window]].wait_send()
                        sent.add(far[-window])
                    far.append((j, e))
                if e == 0:
                    if at >= ahead:
                        send_rows(at, 0)
                elif j > 0:
                    column_copies[j, e].wait_recv()
                    send_rows(at, e)
        if at >= lag:
            encode(at - lag)
            if at > lag:
                decode(at - lag - 1)
    decode(groups - 1)
    for copy in loss_copies:
        copy.wait_recv()
    losses[blk] = jnp.sum(level_losses[...], axis=0)
    for e in range(replicas - 1, 0, -1):
        copy = pltpu.make_async_remote_copy(
            src_ref=losses.at[blk],
            dst_ref=losses.at[blk],
            send_sem=total_send.at[e],
            recv_sem=total_recv.at[e],
            device_id=device(0, e),
            device_id_type=MESH,
        )
        copy.start()
        total_copies.append(copy)

    for j, copy in code_copies:
        if j == 0:
            copy.wait()
        else:
            copy.wait_recv()
    codes_out_ref[...] = jnp.dot(
        placed.T.astype(jnp.bfloat16), returned[...], preferred_element_type=jnp.float32
    ).astype(jnp.bfloat16)

    for copy in total_copies:
        copy.wait_recv()
    total = jnp.sum(losses[...], axis=0)
    loss_ref[...] = jnp.sum(total, keepdims=True) / (
        tok_rows * groups * replicas * features
    )

    for (j, e), copy in row_copies.items():
        if j > 0 and (j, e) not in sent:
            copy.wait_send()
    for copy in column_copies.values():
        copy.wait_send()
    for copy in part_copies + loss_copies + total_copies:
        copy.wait_send()
    for j, copy in code_copies:
        if j > 0:
            copy.wait_send()


def routed(activations, block_ids, enc_weight, enc_bias, dec_weight, dec_bias):
    groups = lax.axis_size("latent")
    replicas = lax.axis_size("blk")
    devices = groups * replicas
    tok_rows, features = activations.shape
    latents = enc_weight.shape[2]
    seg = tok_rows // groups
    width = features // replicas
    tile = math.gcd(512, width)
    vmem = pl.BlockSpec(memory_space=pltpu.VMEM)
    hbm = pl.BlockSpec(memory_space=pltpu.HBM)
    dma = pltpu.SemaphoreType.DMA
    loss, codes, gradient = pl.pallas_call(
        functools.partial(kernel, groups, replicas, tile),
        out_shape=(
            jax.ShapeDtypeStruct((1, 1), jnp.float32),
            jax.ShapeDtypeStruct((tok_rows, latents), jnp.bfloat16),
            jax.ShapeDtypeStruct((1, latents, width), jnp.float32),
        ),
        in_specs=[hbm] * 4,
        out_specs=(vmem, vmem, vmem),
        scratch_shapes=[
            pltpu.VMEM((1, tok_rows + latents + features), jnp.float32),
            pltpu.VMEM((tok_rows, features), jnp.bfloat16),
            pltpu.VMEM((tok_rows, features), jnp.bfloat16),
            pltpu.VMEM((devices * seg, width), jnp.bfloat16),
            pltpu.VMEM((devices * seg, width), jnp.bfloat16),
            pltpu.VMEM((width, latents), jnp.bfloat16),
            pltpu.VMEM((latents, width), jnp.bfloat16),
            pltpu.VMEM((groups, replicas, replicas * seg, latents), jnp.float32),
            pltpu.VMEM((devices * seg, latents), jnp.bfloat16),
            pltpu.VMEM((tok_rows, latents), jnp.bfloat16),
            pltpu.VMEM((8, width), jnp.float32),
            pltpu.VMEM((groups, 8, 128), jnp.float32),
            pltpu.VMEM((replicas, 8, 128), jnp.float32),
            pltpu.VMEM((replicas * seg, width), jnp.bfloat16),
            dma((replicas + 5,)),
            dma((devices,)),
            dma((devices,)),
            dma((devices,)),
            dma((devices,)),
            dma((devices,)),
            dma((devices,)),
            dma((groups,)),
            dma((groups,)),
            dma((groups,)),
            dma((groups,)),
            dma((replicas,)),
            dma((replicas,)),
        ],
        compiler_params=pltpu.CompilerParams(
            collective_id=0, has_side_effects=True, vmem_limit_bytes=52 * 1024 * 1024
        ),
    )(
        jnp.concatenate(
            (block_ids[:, 0].astype(jnp.float32), enc_bias[0], dec_bias)
        ).reshape(1, tok_rows + latents + features),
        activations,
        enc_weight,
        dec_weight,
    )
    return loss[0, 0], codes, gradient


def spread(activations, block_ids, enc_weight, enc_bias, dec_weight, dec_bias):
    groups = lax.axis_size("latent")
    replicas = lax.axis_size("blk")
    tok_rows, features = activations.shape
    per_owner = tok_rows // groups
    block_of = block_ids[:, 0]
    matches = (block_of[:, None] == block_of[None, :]).astype(jnp.int32)
    earlier = jnp.sum(jnp.tril(matches, -1), axis=1)
    placed = block_of * per_owner + earlier
    source_row = (
        jnp.zeros((tok_rows,), jnp.int32).at[placed].set(jnp.arange(tok_rows, dtype=jnp.int32))
    )
    outgoing = activations[source_row]
    contract = (((0,), (0,)), ((), ()))
    incoming = lax.all_to_all(outgoing, "latent", split_axis=0, concat_axis=0, tiled=True)
    centered = (incoming.astype(jnp.float32) - dec_bias).astype(jnp.bfloat16)
    pre_codes = jnp.dot(centered, enc_weight[0], preferred_element_type=jnp.float32) + enc_bias[0]
    codes = jnp.maximum(pre_codes, 0.0).astype(jnp.bfloat16)
    error_rows = (
        jnp.dot(codes, dec_weight[0], preferred_element_type=jnp.float32)
        + dec_bias
        - incoming.astype(jnp.float32)
    )
    squares = jnp.sum(error_rows * error_rows)
    partial_grad = lax.dot_general(
        codes, error_rows.astype(jnp.bfloat16), contract, preferred_element_type=jnp.float32
    )
    summed = lax.psum_scatter(
        partial_grad.astype(jnp.bfloat16), "blk", scatter_dimension=1, tiled=True
    ).astype(jnp.float32)
    returned = lax.all_to_all(codes, "latent", split_axis=0, concat_axis=0, tiled=True)
    token_codes = returned[placed]
    gradient = summed / (tok_rows * replicas)
    summed_loss = lax.psum(squares, ("latent", "blk"))
    loss_value = summed_loss / (tok_rows * groups * replicas * features)
    return (loss_value, token_codes, gradient[None])


def solution(mesh):
    groups, replicas = mesh.shape["latent"], mesh.shape["blk"]
    placed = (
        P(("latent", "blk"), None),
        P(("latent", "blk"), None),
        P("latent", None, None),
        P("latent", None),
        P("latent", None, None),
        P(),
    )

    def local(activations, *rest):
        tok_rows, features = activations.shape
        fits = (
            groups & (groups - 1) == 0
            and replicas & (replicas - 1) == 0
            and 1 < groups <= tok_rows
            and tok_rows % 128 == 0
            and tok_rows % (16 * groups) == 0
            and rest[1].shape[2] % 128 == 0
            and features % (128 * replicas) == 0
        )
        return (routed if fits else spread)(activations, *rest)

    return jax.shard_map(
        local,
        mesh=mesh,
        in_specs=placed,
        out_specs=(P(), P(("latent", "blk"), None), P("latent", None, "blk")),
        check_vma=False,
    )
```

```python
import functools
import math

import jax
import jax.numpy as jnp
from jax import lax
from jax.experimental import pallas as pl
from jax.experimental.pallas import tpu as pltpu
from jax.sharding import PartitionSpec as P

MESH = pl.DeviceIdType.MESH


def flip(index, mask):
    out, bit = index, 1
    while bit <= mask:
        if mask & bit:
            out = out + bit * (1 - 2 * ((index // bit) % 2))
        bit *= 2
    return out


def kernel(
    groups,
    replicas,
    tile,
    small_hbm,
    act_hbm,
    enc_hbm,
    dec_hbm,
    loss_ref,
    codes_out_ref,
    grad_ref,
    small,
    act,
    ordered,
    staged,
    arrived,
    enc,
    dec,
    parts,
    codes,
    returned,
    squares,
    level_losses,
    losses,
    error_low,
    load_sem,
    row_send,
    row_recv,
    column_send,
    column_recv,
    part_send,
    part_recv,
    code_send,
    code_recv,
    loss_send,
    loss_recv,
    total_send,
    total_recv,
):
    lat, blk = lax.axis_index("latent"), lax.axis_index("blk")
    tok_rows, features = act.shape
    seg = tok_rows // groups
    width = features // replicas
    latents = enc.shape[1]
    tiles = width // tile
    group_rows = replicas * seg
    own_cols = pl.multiple_of(blk * width, width)
    bias_at = tok_rows + latents + own_cols
    order = list(range(groups // 2 - 1, -1, -1)) + list(range(groups // 2, groups))
    turns = [at for i in range(groups // 2) for at in (groups // 2 + i, i)]
    peers = [(j, 0) for j in range(1, groups)] + [(0, e) for e in range(1, replicas)]

    def device(j, e):
        return (flip(lat, j), flip(blk, e))

    barrier = pltpu.get_barrier_semaphore()
    load_small = pltpu.make_async_copy(small_hbm, small, load_sem.at[replicas + 2])
    load_small.start()
    loads = []
    for e in range(replicas):
        cols = pl.ds(pl.multiple_of(flip(blk, e) * width, width), width)
        loads.append(
            pltpu.make_async_copy(act_hbm.at[:, cols], act.at[:, cols], load_sem.at[e])
        )
    load_enc = pltpu.make_async_copy(
        enc_hbm.at[0, pl.ds(own_cols, width), :], enc, load_sem.at[replicas]
    )
    load_dec = pltpu.make_async_copy(
        dec_hbm.at[0, :, pl.ds(own_cols, width)], dec, load_sem.at[replicas + 1]
    )
    for load in loads:
        load.start()
    for j, e in reversed(peers):
        pl.semaphore_signal(barrier, inc=1, device_id=device(j, e), device_id_type=MESH)
    load_enc.start()
    load_dec.start()
    load_small.wait()

    ids = small[:, :tok_rows]
    square = (tok_rows, tok_rows)
    down = lax.broadcasted_iota(jnp.int32, square, 0)
    along = lax.broadcasted_iota(jnp.int32, square, 1)
    named = (ids == down.astype(jnp.float32)).astype(jnp.float32)
    earlier = jnp.dot(
        named.astype(jnp.bfloat16),
        (down < along).astype(jnp.float32).astype(jnp.bfloat16),
        preferred_element_type=jnp.float32,
    )
    place = jnp.sum(named * earlier, axis=0, keepdims=True) + ids * seg
    placed = (place == down.astype(jnp.float32)).astype(jnp.float32)
    to_place = placed.astype(jnp.bfloat16)

    row_copies, column_copies = {}, {}

    def piece(j, e):
        return (
            pl.ds(pl.multiple_of(flip(lat, j) * seg, seg), seg),
            pl.ds(pl.multiple_of(flip(blk, e) * width, width), width),
        )

    def place_at(at, e):
        return pl.ds(pl.multiple_of((at * replicas + flip(blk, e)) * seg, seg), seg)

    def send_rows(at, e):
        j = order[at]
        target = arrived.at[place_at(at, e), :]
        source = ordered.at[piece(j, e)] if e == 0 else staged.at[place_at(at, e), :]
        if j == 0:
            copy = pltpu.make_async_copy(source, target, row_recv.at[0])
        else:
            copy = pltpu.make_async_remote_copy(
                src_ref=source,
                dst_ref=target,
                send_sem=row_send.at[j * replicas + e],
                recv_sem=row_recv.at[j * replicas + e],
                device_id=device(j, 0),
                device_id_type=MESH,
            )
        copy.start()
        row_copies[j, e] = copy

    def send_columns(at, e):
        j = order[at]
        landing = arrived if j == 0 else staged
        copy = pltpu.make_async_remote_copy(
            src_ref=ordered.at[piece(j, e)],
            dst_ref=landing.at[place_at(at, 0), :],
            send_sem=column_send.at[j * replicas + e],
            recv_sem=column_recv.at[j * replicas + e],
            device_id=device(0, e),
            device_id_type=MESH,
        )
        copy.start()
        column_copies[j, e] = copy

    for e in range(replicas):
        loads[e].wait()

        def order_rows(i, carry):
            cols = pl.ds(pl.multiple_of(flip(blk, e) * width + i * tile, tile), tile)
            ordered[:, cols] = jnp.dot(
                to_place, act[:, cols], preferred_element_type=jnp.float32
            ).astype(jnp.bfloat16)
            return carry

        lax.fori_loop(0, tiles, order_rows, 0, unroll=True)
        if e == 0:
            pl.semaphore_wait(barrier, len(peers))
            for at in turns:
                send_rows(at, 0)
    for at in turns:
        for e in range(1, replicas):
            send_columns(at, e)
    for at in turns:
        if order[at] > 0:
            for e in range(1, replicas):
                column_copies[order[at], e].wait_recv()
                send_rows(at, e)

    load_enc.wait()
    load_dec.wait()
    squares[...] = jnp.zeros_like(squares)
    part_copies, code_copies = [], []

    def encode(at):
        for e in range(replicas):
            if (order[at], e) == (0, 0):
                row_copies[0, 0].wait()
            elif order[at] == 0:
                column_copies[0, e].wait_recv()
            else:
                row_copies[order[at], e].wait_recv()

        def step(i, total):
            cols = pl.ds(pl.multiple_of(i * tile, tile), tile)
            bias = small[:, pl.ds(pl.multiple_of(bias_at + i * tile, 128), tile)]
            rows = arrived[pl.ds(at * group_rows, group_rows), cols]
            centered = (rows.astype(jnp.float32) - bias).astype(jnp.bfloat16)
            return total + jnp.dot(centered, enc[cols, :], preferred_element_type=jnp.float32)

        parts[at, blk] = lax.fori_loop(
            0, tiles, step, jnp.zeros((group_rows, latents), jnp.float32), unroll=True
        )
        for e in range(1, replicas):
            copy = pltpu.make_async_remote_copy(
                src_ref=parts.at[at, blk],
                dst_ref=parts.at[at, blk],
                send_sem=part_send.at[at * replicas + e],
                recv_sem=part_recv.at[at * replicas + e],
                device_id=device(0, e),
                device_id_type=MESH,
            )
            copy.start()
            part_copies.append(copy)

    def decode(at):
        for copy in part_copies[at * (replicas - 1) : (at + 1) * (replicas - 1)]:
            copy.wait_recv()
        total = parts[at, 0]
        for d in range(1, replicas):
            total = total + parts[at, d]
        wide = jnp.maximum(total + small[:, tok_rows : tok_rows + latents], 0.0)
        low = wide.astype(jnp.bfloat16)
        flipped = low.astype(jnp.float32).T.astype(jnp.bfloat16)
        codes[pl.ds(at * group_rows, group_rows), :] = low
        j = order[at]
        home = pl.ds(pl.multiple_of(lat * seg, seg), seg)
        source = codes.at[pl.ds(pl.multiple_of((at * replicas + blk) * seg, seg), seg), :]
        if j == 0:
            copy = pltpu.make_async_copy(source, returned.at[home, :], code_recv.at[0])
        else:
            copy = pltpu.make_async_remote_copy(
                src_ref=source,
                dst_ref=returned.at[home, :],
                send_sem=code_send.at[j],
                recv_sem=code_recv.at[j],
                device_id=device(j, 0),
                device_id_type=MESH,
            )
        copy.start()
        code_copies.append((j, copy))

        def errors(i, carry):
            cols = pl.ds(pl.multiple_of(i * tile, tile), tile)
            bias = small[:, pl.ds(pl.multiple_of(bias_at + i * tile, 128), tile)]
            rows = arrived[pl.ds(at * group_rows, group_rows), cols]
            error = (
                jnp.dot(low, dec[:, cols], preferred_element_type=jnp.float32)
                + bias
                - rows.astype(jnp.float32)
            )
            squares[:, cols] += jnp.sum(
                (error * error).reshape(group_rows // 8, 8, tile), axis=0
            )
            error_low[:, cols] = error.astype(jnp.bfloat16)
            return carry

        def gradient(i, carry):
            cols = pl.ds(pl.multiple_of(i * tile, tile), tile)
            term = jnp.dot(flipped, error_low[:, cols], preferred_element_type=jnp.float32)
            if at > 0:
                term = grad_ref[0, :, cols] + term
            if at == groups - 1:
                term = term / (tok_rows * replicas)
            grad_ref[0, :, cols] = term
            return carry

        lax.fori_loop(0, tiles, errors, 0, unroll=True)
        if at == groups - 1:
            send_squares()
        lax.fori_loop(0, tiles, gradient, 0, unroll=True)

    loss_copies, total_copies = [], []

    def send_squares():
        own = squares[:, :128]
        for i in range(1, width // 128):
            own = own + squares[:, i * 128 : (i + 1) * 128]
        level_losses[lat] = own
        for j in range(groups - 1, 0, -1):
            copy = pltpu.make_async_remote_copy(
                src_ref=level_losses.at[lat],
                dst_ref=level_losses.at[lat],
                send_sem=loss_send.at[j],
                recv_sem=loss_recv.at[j],
                device_id=device(j, 0),
                device_id_type=MESH,
            )
            copy.start()
            loss_copies.append(copy)

    for at in range(groups):
        encode(at)
        if at > 0:
            decode(at - 1)
    decode(groups - 1)
    for copy in loss_copies:
        copy.wait_recv()
    losses[blk] = jnp.sum(level_losses[...], axis=0)
    for e in range(replicas - 1, 0, -1):
        copy = pltpu.make_async_remote_copy(
            src_ref=losses.at[blk],
            dst_ref=losses.at[blk],
            send_sem=total_send.at[e],
            recv_sem=total_recv.at[e],
            device_id=device(0, e),
            device_id_type=MESH,
        )
        copy.start()
        total_copies.append(copy)

    for j, copy in code_copies:
        if j == 0:
            copy.wait()
        else:
            copy.wait_recv()
    codes_out_ref[...] = jnp.dot(
        placed.T.astype(jnp.bfloat16), returned[...], preferred_element_type=jnp.float32
    ).astype(jnp.bfloat16)

    for copy in total_copies:
        copy.wait_recv()
    total = jnp.sum(losses[...], axis=0)
    loss_ref[...] = jnp.sum(total, keepdims=True) / (
        tok_rows * groups * replicas * features
    )

    for (j, e), copy in row_copies.items():
        if j > 0:
            copy.wait_send()
    for copy in column_copies.values():
        copy.wait_send()
    for copy in part_copies + loss_copies + total_copies:
        copy.wait_send()
    for j, copy in code_copies:
        if j > 0:
            copy.wait_send()


def routed(activations, block_ids, enc_weight, enc_bias, dec_weight, dec_bias):
    groups = lax.axis_size("latent")
    replicas = lax.axis_size("blk")
    devices = groups * replicas
    tok_rows, features = activations.shape
    latents = enc_weight.shape[2]
    seg = tok_rows // groups
    width = features // replicas
    tile = math.gcd(512, width)
    vmem = pl.BlockSpec(memory_space=pltpu.VMEM)
    hbm = pl.BlockSpec(memory_space=pltpu.HBM)
    dma = pltpu.SemaphoreType.DMA
    loss, codes, gradient = pl.pallas_call(
        functools.partial(kernel, groups, replicas, tile),
        out_shape=(
            jax.ShapeDtypeStruct((1, 1), jnp.float32),
            jax.ShapeDtypeStruct((tok_rows, latents), jnp.bfloat16),
            jax.ShapeDtypeStruct((1, latents, width), jnp.float32),
        ),
        in_specs=[hbm] * 4,
        out_specs=(vmem, vmem, vmem),
        scratch_shapes=[
            pltpu.VMEM((1, tok_rows + latents + features), jnp.float32),
            pltpu.VMEM((tok_rows, features), jnp.bfloat16),
            pltpu.VMEM((tok_rows, features), jnp.bfloat16),
            pltpu.VMEM((devices * seg, width), jnp.bfloat16),
            pltpu.VMEM((devices * seg, width), jnp.bfloat16),
            pltpu.VMEM((width, latents), jnp.bfloat16),
            pltpu.VMEM((latents, width), jnp.bfloat16),
            pltpu.VMEM((groups, replicas, replicas * seg, latents), jnp.float32),
            pltpu.VMEM((devices * seg, latents), jnp.bfloat16),
            pltpu.VMEM((tok_rows, latents), jnp.bfloat16),
            pltpu.VMEM((8, width), jnp.float32),
            pltpu.VMEM((groups, 8, 128), jnp.float32),
            pltpu.VMEM((replicas, 8, 128), jnp.float32),
            pltpu.VMEM((replicas * seg, width), jnp.bfloat16),
            dma((replicas + 5,)),
            dma((devices,)),
            dma((devices,)),
            dma((devices,)),
            dma((devices,)),
            dma((devices,)),
            dma((devices,)),
            dma((groups,)),
            dma((groups,)),
            dma((groups,)),
            dma((groups,)),
            dma((replicas,)),
            dma((replicas,)),
        ],
        compiler_params=pltpu.CompilerParams(
            collective_id=0, has_side_effects=True, vmem_limit_bytes=52 * 1024 * 1024
        ),
    )(
        jnp.concatenate(
            (block_ids[:, 0].astype(jnp.float32), enc_bias[0], dec_bias)
        ).reshape(1, tok_rows + latents + features),
        activations,
        enc_weight,
        dec_weight,
    )
    return loss[0, 0], codes, gradient


def spread(activations, block_ids, enc_weight, enc_bias, dec_weight, dec_bias):
    groups = lax.axis_size("latent")
    replicas = lax.axis_size("blk")
    tok_rows, features = activations.shape
    per_owner = tok_rows // groups
    block_of = block_ids[:, 0]
    matches = (block_of[:, None] == block_of[None, :]).astype(jnp.int32)
    earlier = jnp.sum(jnp.tril(matches, -1), axis=1)
    placed = block_of * per_owner + earlier
    source_row = (
        jnp.zeros((tok_rows,), jnp.int32).at[placed].set(jnp.arange(tok_rows, dtype=jnp.int32))
    )
    outgoing = activations[source_row]
    contract = (((0,), (0,)), ((), ()))
    incoming = lax.all_to_all(outgoing, "latent", split_axis=0, concat_axis=0, tiled=True)
    centered = (incoming.astype(jnp.float32) - dec_bias).astype(jnp.bfloat16)
    pre_codes = jnp.dot(centered, enc_weight[0], preferred_element_type=jnp.float32) + enc_bias[0]
    codes = jnp.maximum(pre_codes, 0.0).astype(jnp.bfloat16)
    error_rows = (
        jnp.dot(codes, dec_weight[0], preferred_element_type=jnp.float32)
        + dec_bias
        - incoming.astype(jnp.float32)
    )
    squares = jnp.sum(error_rows * error_rows)
    partial_grad = lax.dot_general(
        codes, error_rows.astype(jnp.bfloat16), contract, preferred_element_type=jnp.float32
    )
    summed = lax.psum_scatter(
        partial_grad.astype(jnp.bfloat16), "blk", scatter_dimension=1, tiled=True
    ).astype(jnp.float32)
    returned = lax.all_to_all(codes, "latent", split_axis=0, concat_axis=0, tiled=True)
    token_codes = returned[placed]
    gradient = summed / (tok_rows * replicas)
    summed_loss = lax.psum(squares, ("latent", "blk"))
    loss_value = summed_loss / (tok_rows * groups * replicas * features)
    return (loss_value, token_codes, gradient[None])


def solution(mesh):
    groups, replicas = mesh.shape["latent"], mesh.shape["blk"]
    placed = (
        P(("latent", "blk"), None),
        P(("latent", "blk"), None),
        P("latent", None, None),
        P("latent", None),
        P("latent", None, None),
        P(),
    )

    def local(activations, *rest):
        tok_rows, features = activations.shape
        fits = (
            groups & (groups - 1) == 0
            and replicas & (replicas - 1) == 0
            and 1 < groups <= tok_rows
            and tok_rows % 128 == 0
            and tok_rows % (16 * groups) == 0
            and rest[1].shape[2] % 128 == 0
            and features % (128 * replicas) == 0
        )
        return (routed if fits else spread)(activations, *rest)

    return jax.shard_map(
        local,
        mesh=mesh,
        in_specs=placed,
        out_specs=(P(), P(("latent", "blk"), None), P("latent", None, "blk")),
        check_vma=False,
    )
```

```python
import functools
import math

import jax
import jax.numpy as jnp
from jax import lax
from jax.experimental import pallas as pl
from jax.experimental.pallas import tpu as pltpu
from jax.sharding import PartitionSpec as P

MESH = pl.DeviceIdType.MESH


def flip(index, mask):
    out, bit = index, 1
    while bit <= mask:
        if mask & bit:
            out = out + bit * (1 - 2 * ((index // bit) % 2))
        bit *= 2
    return out


def kernel(
    groups,
    replicas,
    tile,
    small_hbm,
    act_hbm,
    enc_hbm,
    dec_hbm,
    loss_ref,
    codes_out_ref,
    grad_ref,
    small,
    act,
    ordered,
    staged,
    arrived,
    enc,
    dec,
    parts,
    codes,
    returned,
    squares,
    level_losses,
    losses,
    error_low,
    load_sem,
    row_send,
    row_recv,
    column_send,
    column_recv,
    part_send,
    part_recv,
    code_send,
    code_recv,
    loss_send,
    loss_recv,
    total_send,
    total_recv,
):
    lat, blk = lax.axis_index("latent"), lax.axis_index("blk")
    tok_rows, features = act.shape
    seg = tok_rows // groups
    width = features // replicas
    latents = enc.shape[1]
    tiles = width // tile
    group_rows = replicas * seg
    own_cols = pl.multiple_of(blk * width, width)
    bias_at = tok_rows + latents + own_cols
    order = list(range(groups // 2 - 1, -1, -1)) + list(range(groups // 2, groups))
    turns = [at for i in range(groups // 2) for at in (groups // 2 + i, i)]
    peers = [(j, 0) for j in range(1, groups)] + [(0, e) for e in range(1, replicas)]

    def device(j, e):
        return (flip(lat, j), flip(blk, e))

    barrier = pltpu.get_barrier_semaphore()
    load_small = pltpu.make_async_copy(small_hbm, small, load_sem.at[replicas + 2])
    load_small.start()
    loads = []
    for e in range(replicas):
        cols = pl.ds(pl.multiple_of(flip(blk, e) * width, width), width)
        loads.append(
            pltpu.make_async_copy(act_hbm.at[:, cols], act.at[:, cols], load_sem.at[e])
        )
    load_enc = pltpu.make_async_copy(
        enc_hbm.at[0, pl.ds(own_cols, width), :], enc, load_sem.at[replicas]
    )
    load_dec = pltpu.make_async_copy(
        dec_hbm.at[0, :, pl.ds(own_cols, width)], dec, load_sem.at[replicas + 1]
    )
    for load in loads:
        load.start()
    for j, e in reversed(peers):
        pl.semaphore_signal(barrier, inc=1, device_id=device(j, e), device_id_type=MESH)
    load_enc.start()
    load_dec.start()
    load_small.wait()

    ids = small[:, :tok_rows]
    square = (tok_rows, tok_rows)
    down = lax.broadcasted_iota(jnp.int32, square, 0)
    along = lax.broadcasted_iota(jnp.int32, square, 1)
    named = (ids == down.astype(jnp.float32)).astype(jnp.float32)
    earlier = jnp.dot(
        named.astype(jnp.bfloat16),
        (down < along).astype(jnp.float32).astype(jnp.bfloat16),
        preferred_element_type=jnp.float32,
    )
    place = jnp.sum(named * earlier, axis=0, keepdims=True) + ids * seg
    placed = (place == down.astype(jnp.float32)).astype(jnp.float32)
    to_place = placed.astype(jnp.bfloat16)

    row_copies, column_copies = {}, {}

    def piece(j, e):
        return (
            pl.ds(pl.multiple_of(flip(lat, j) * seg, seg), seg),
            pl.ds(pl.multiple_of(flip(blk, e) * width, width), width),
        )

    def place_at(at, e):
        return pl.ds(pl.multiple_of((at * replicas + flip(blk, e)) * seg, seg), seg)

    def send_rows(at, e):
        j = order[at]
        target = arrived.at[place_at(at, e), :]
        source = ordered.at[piece(j, e)] if e == 0 else staged.at[place_at(at, e), :]
        if j == 0:
            copy = pltpu.make_async_copy(source, target, row_recv.at[0])
        else:
            copy = pltpu.make_async_remote_copy(
                src_ref=source,
                dst_ref=target,
                send_sem=row_send.at[j * replicas + e],
                recv_sem=row_recv.at[j * replicas + e],
                device_id=device(j, 0),
                device_id_type=MESH,
            )
        copy.start()
        row_copies[j, e] = copy

    def send_columns(at, e):
        j = order[at]
        landing = arrived if j == 0 else staged
        copy = pltpu.make_async_remote_copy(
            src_ref=ordered.at[piece(j, e)],
            dst_ref=landing.at[place_at(at, 0), :],
            send_sem=column_send.at[j * replicas + e],
            recv_sem=column_recv.at[j * replicas + e],
            device_id=device(0, e),
            device_id_type=MESH,
        )
        copy.start()
        column_copies[j, e] = copy

    for e in range(replicas):
        loads[e].wait()

        def order_rows(i, carry):
            cols = pl.ds(pl.multiple_of(flip(blk, e) * width + i * tile, tile), tile)
            ordered[:, cols] = jnp.dot(
                to_place, act[:, cols], preferred_element_type=jnp.float32
            ).astype(jnp.bfloat16)
            return carry

        lax.fori_loop(0, tiles, order_rows, 0, unroll=True)
        if e == 0:
            pl.semaphore_wait(barrier, len(peers))
            for at in turns:
                send_rows(at, 0)
    for at in turns:
        for e in range(1, replicas):
            send_columns(at, e)
    for at in turns:
        if order[at] > 0:
            for e in range(1, replicas):
                column_copies[order[at], e].wait_recv()
                send_rows(at, e)

    load_enc.wait()
    load_dec.wait()
    squares[...] = jnp.zeros_like(squares)
    part_copies, code_copies = [], []

    def encode(at):
        for e in range(replicas):
            if (order[at], e) == (0, 0):
                row_copies[0, 0].wait()
            elif order[at] == 0:
                column_copies[0, e].wait_recv()
            else:
                row_copies[order[at], e].wait_recv()

        def step(i, total):
            cols = pl.ds(pl.multiple_of(i * tile, tile), tile)
            bias = small[:, pl.ds(pl.multiple_of(bias_at + i * tile, 128), tile)]
            rows = arrived[pl.ds(at * group_rows, group_rows), cols]
            centered = (rows.astype(jnp.float32) - bias).astype(jnp.bfloat16)
            return total + jnp.dot(centered, enc[cols, :], preferred_element_type=jnp.float32)

        parts[at, blk] = lax.fori_loop(
            0, tiles, step, jnp.zeros((group_rows, latents), jnp.float32), unroll=True
        )
        for e in range(1, replicas):
            copy = pltpu.make_async_remote_copy(
                src_ref=parts.at[at, blk],
                dst_ref=parts.at[at, blk],
                send_sem=part_send.at[at * replicas + e],
                recv_sem=part_recv.at[at * replicas + e],
                device_id=device(0, e),
                device_id_type=MESH,
            )
            copy.start()
            part_copies.append(copy)

    def decode(at):
        for copy in part_copies[at * (replicas - 1) : (at + 1) * (replicas - 1)]:
            copy.wait_recv()
        total = parts[at, 0]
        for d in range(1, replicas):
            total = total + parts[at, d]
        wide = jnp.maximum(total + small[:, tok_rows : tok_rows + latents], 0.0)
        low = wide.astype(jnp.bfloat16)
        codes[pl.ds(at * group_rows, group_rows), :] = low
        j = order[at]
        home = pl.ds(pl.multiple_of(lat * seg, seg), seg)
        source = codes.at[pl.ds(pl.multiple_of((at * replicas + blk) * seg, seg), seg), :]
        if j == 0:
            copy = pltpu.make_async_copy(source, returned.at[home, :], code_recv.at[0])
        else:
            copy = pltpu.make_async_remote_copy(
                src_ref=source,
                dst_ref=returned.at[home, :],
                send_sem=code_send.at[j],
                recv_sem=code_recv.at[j],
                device_id=device(j, 0),
                device_id_type=MESH,
            )
        copy.start()
        code_copies.append((j, copy))

        def errors(i, carry):
            cols = pl.ds(pl.multiple_of(i * tile, tile), tile)
            bias = small[:, pl.ds(pl.multiple_of(bias_at + i * tile, 128), tile)]
            rows = arrived[pl.ds(at * group_rows, group_rows), cols]
            error = (
                jnp.dot(low, dec[:, cols], preferred_element_type=jnp.float32)
                + bias
                - rows.astype(jnp.float32)
            )
            squares[:, cols] += jnp.sum(
                (error * error).reshape(group_rows // 8, 8, tile), axis=0
            )
            error_low[pl.ds(at * group_rows, group_rows), cols] = error.astype(jnp.bfloat16)
            return carry

        lax.fori_loop(0, tiles, errors, 0, unroll=True)
        if at == groups - 1:
            send_squares()

    loss_copies, total_copies = [], []

    def send_squares():
        own = squares[:, :128]
        for i in range(1, width // 128):
            own = own + squares[:, i * 128 : (i + 1) * 128]
        level_losses[lat] = own
        for j in range(groups - 1, 0, -1):
            copy = pltpu.make_async_remote_copy(
                src_ref=level_losses.at[lat],
                dst_ref=level_losses.at[lat],
                send_sem=loss_send.at[j],
                recv_sem=loss_recv.at[j],
                device_id=device(j, 0),
                device_id_type=MESH,
            )
            copy.start()
            loss_copies.append(copy)

    for at in range(groups):
        encode(at)
        if at > 0:
            decode(at - 1)
    decode(groups - 1)

    flipped = codes[...].astype(jnp.float32).T.astype(jnp.bfloat16)

    def gradient(i, carry):
        cols = pl.ds(pl.multiple_of(i * tile, tile), tile)
        term = jnp.dot(flipped, error_low[:, cols], preferred_element_type=jnp.float32)
        grad_ref[0, :, cols] = term / (tok_rows * replicas)
        return carry

    lax.fori_loop(0, tiles // 2, gradient, 0, unroll=True)
    for copy in loss_copies:
        copy.wait_recv()
    losses[blk] = jnp.sum(level_losses[...], axis=0)
    for e in range(replicas - 1, 0, -1):
        copy = pltpu.make_async_remote_copy(
            src_ref=losses.at[blk],
            dst_ref=losses.at[blk],
            send_sem=total_send.at[e],
            recv_sem=total_recv.at[e],
            device_id=device(0, e),
            device_id_type=MESH,
        )
        copy.start()
        total_copies.append(copy)
    lax.fori_loop(tiles // 2, tiles, gradient, 0, unroll=True)

    for j, copy in code_copies:
        if j == 0:
            copy.wait()
        else:
            copy.wait_recv()
    codes_out_ref[...] = jnp.dot(
        placed.T.astype(jnp.bfloat16), returned[...], preferred_element_type=jnp.float32
    ).astype(jnp.bfloat16)

    for copy in total_copies:
        copy.wait_recv()
    total = jnp.sum(losses[...], axis=0)
    loss_ref[...] = jnp.sum(total, keepdims=True) / (
        tok_rows * groups * replicas * features
    )

    for (j, e), copy in row_copies.items():
        if j > 0:
            copy.wait_send()
    for copy in column_copies.values():
        copy.wait_send()
    for copy in part_copies + loss_copies + total_copies:
        copy.wait_send()
    for j, copy in code_copies:
        if j > 0:
            copy.wait_send()


def routed(activations, block_ids, enc_weight, enc_bias, dec_weight, dec_bias):
    groups = lax.axis_size("latent")
    replicas = lax.axis_size("blk")
    devices = groups * replicas
    tok_rows, features = activations.shape
    latents = enc_weight.shape[2]
    seg = tok_rows // groups
    width = features // replicas
    tile = math.gcd(512, width)
    vmem = pl.BlockSpec(memory_space=pltpu.VMEM)
    hbm = pl.BlockSpec(memory_space=pltpu.HBM)
    dma = pltpu.SemaphoreType.DMA
    loss, codes, gradient = pl.pallas_call(
        functools.partial(kernel, groups, replicas, tile),
        out_shape=(
            jax.ShapeDtypeStruct((1, 1), jnp.float32),
            jax.ShapeDtypeStruct((tok_rows, latents), jnp.bfloat16),
            jax.ShapeDtypeStruct((1, latents, width), jnp.float32),
        ),
        in_specs=[hbm] * 4,
        out_specs=(vmem, vmem, vmem),
        scratch_shapes=[
            pltpu.VMEM((1, tok_rows + latents + features), jnp.float32),
            pltpu.VMEM((tok_rows, features), jnp.bfloat16),
            pltpu.VMEM((tok_rows, features), jnp.bfloat16),
            pltpu.VMEM((devices * seg, width), jnp.bfloat16),
            pltpu.VMEM((devices * seg, width), jnp.bfloat16),
            pltpu.VMEM((width, latents), jnp.bfloat16),
            pltpu.VMEM((latents, width), jnp.bfloat16),
            pltpu.VMEM((groups, replicas, replicas * seg, latents), jnp.float32),
            pltpu.VMEM((devices * seg, latents), jnp.bfloat16),
            pltpu.VMEM((tok_rows, latents), jnp.bfloat16),
            pltpu.VMEM((8, width), jnp.float32),
            pltpu.VMEM((groups, 8, 128), jnp.float32),
            pltpu.VMEM((replicas, 8, 128), jnp.float32),
            pltpu.VMEM((devices * seg, width), jnp.bfloat16),
            dma((replicas + 5,)),
            dma((devices,)),
            dma((devices,)),
            dma((devices,)),
            dma((devices,)),
            dma((devices,)),
            dma((devices,)),
            dma((groups,)),
            dma((groups,)),
            dma((groups,)),
            dma((groups,)),
            dma((replicas,)),
            dma((replicas,)),
        ],
        compiler_params=pltpu.CompilerParams(
            collective_id=0, has_side_effects=True, vmem_limit_bytes=52 * 1024 * 1024
        ),
    )(
        jnp.concatenate(
            (block_ids[:, 0].astype(jnp.float32), enc_bias[0], dec_bias)
        ).reshape(1, tok_rows + latents + features),
        activations,
        enc_weight,
        dec_weight,
    )
    return loss[0, 0], codes, gradient


def spread(activations, block_ids, enc_weight, enc_bias, dec_weight, dec_bias):
    groups = lax.axis_size("latent")
    replicas = lax.axis_size("blk")
    tok_rows, features = activations.shape
    per_owner = tok_rows // groups
    block_of = block_ids[:, 0]
    matches = (block_of[:, None] == block_of[None, :]).astype(jnp.int32)
    earlier = jnp.sum(jnp.tril(matches, -1), axis=1)
    placed = block_of * per_owner + earlier
    source_row = (
        jnp.zeros((tok_rows,), jnp.int32).at[placed].set(jnp.arange(tok_rows, dtype=jnp.int32))
    )
    outgoing = activations[source_row]
    contract = (((0,), (0,)), ((), ()))
    incoming = lax.all_to_all(outgoing, "latent", split_axis=0, concat_axis=0, tiled=True)
    centered = (incoming.astype(jnp.float32) - dec_bias).astype(jnp.bfloat16)
    pre_codes = jnp.dot(centered, enc_weight[0], preferred_element_type=jnp.float32) + enc_bias[0]
    codes = jnp.maximum(pre_codes, 0.0).astype(jnp.bfloat16)
    error_rows = (
        jnp.dot(codes, dec_weight[0], preferred_element_type=jnp.float32)
        + dec_bias
        - incoming.astype(jnp.float32)
    )
    squares = jnp.sum(error_rows * error_rows)
    partial_grad = lax.dot_general(
        codes, error_rows.astype(jnp.bfloat16), contract, preferred_element_type=jnp.float32
    )
    summed = lax.psum_scatter(
        partial_grad.astype(jnp.bfloat16), "blk", scatter_dimension=1, tiled=True
    ).astype(jnp.float32)
    returned = lax.all_to_all(codes, "latent", split_axis=0, concat_axis=0, tiled=True)
    token_codes = returned[placed]
    gradient = summed / (tok_rows * replicas)
    summed_loss = lax.psum(squares, ("latent", "blk"))
    loss_value = summed_loss / (tok_rows * groups * replicas * features)
    return (loss_value, token_codes, gradient[None])


def solution(mesh):
    groups, replicas = mesh.shape["latent"], mesh.shape["blk"]
    placed = (
        P(("latent", "blk"), None),
        P(("latent", "blk"), None),
        P("latent", None, None),
        P("latent", None),
        P("latent", None, None),
        P(),
    )

    def local(activations, *rest):
        tok_rows, features = activations.shape
        fits = (
            groups & (groups - 1) == 0
            and replicas & (replicas - 1) == 0
            and 1 < groups <= tok_rows
            and tok_rows % 128 == 0
            and tok_rows % (16 * groups) == 0
            and rest[1].shape[2] % 128 == 0
            and features % (128 * replicas) == 0
        )
        return (routed if fits else spread)(activations, *rest)

    return jax.shard_map(
        local,
        mesh=mesh,
        in_specs=placed,
        out_specs=(P(), P(("latent", "blk"), None), P("latent", None, "blk")),
        check_vma=False,
    )
```
